32 devices in a mesh: grp: 2 (over x), tm: 16 (over z, y, core).
Axes of the slice: x: 2, y: 2, z: 4, core: 2. Of those that a mesh axis runs over, the one named last changes fastest.
Arguments:
- dyn_a: float32 [128, 4, 64, 64], P('tm', 'grp'), parts along dimension 1, may hold values from -1 to 1
- dyn_b: float32 [128, 4, 64, 32], P('tm', 'grp'), parts along dimension 1, may hold values from -0.109375 to 0.109375
- gains: float32 [128, 4, 32, 64], P('tm', 'grp'), parts along dimension 1, may hold values from -0.2 to 0.2
- defects: float32 [128, 4, 64], P('tm', 'grp'), parts along dimension 1, may hold values from -6 to 6
- state_grad: float32 [128, 4, 64], P('tm', 'grp'), parts along dimension 1, may hold values from -6 to 6
- control_grad: float32 [128, 4, 32], P('tm', 'grp'), parts along dimension 1, may hold values from -1.5 to 1.5
- cost_factor: float32 [64, 64], replicated, may hold values from -0.75 to 0.75
- control_factor: float32 [32, 32], replicated, may hold values from -1 to 1
- init_state: float32 [4, 64], P('grp'), parts along dimension 0, may hold values from -6 to 6
Outputs:
- new_gains: float32 [128, 4, 32, 64], P('tm', 'grp'), parts along dimension 1
- feedforward: float32 [128, 4, 32], P('tm', 'grp'), parts along dimension 1
- states: float32 [128, 4, 64], P('tm', 'grp'), parts along dimension 1
- controls: float32 [128, 4, 32], P('tm', 'grp'), parts along dimension 1
- decrease: float32 [4], P('grp'), parts along dimension 0
The draws below stay inside these ranges and needn't reach their ends.
There are 2 independent parts, one for each index of `grp`. The reference program is written for one: setup_inputs(seed, part) draws one part's arguments, and reference() takes and returns one part's arrays. A program takes and returns all parts, laid end to end along the dimension named above; an argument that names none is the same for every part. Nothing has to cross between parts.
All inputs are finite; a program needn't handle non-finite values.
Results may differ from the reference program's by a relative error of at most 0.0003.
Values sent between devices are 32-bit elements; how exact they have to be, the bound alone decides.
No kernel may reach another device: no remote copies, remote signals or barrier semaphores. Data moves between devices by JAX's collectives and lax.ppermute only.
A program may use at most 64 MiB of HBM per device.

```python
import math
import jax
import jax.numpy as jnp
from jax import lax

STATE_DIM = 64
NU = 32
TRAJECTORY_COUNT = 2
HORIZON_KNOTS = 128


def draw_dyn_a(key, part):
    random_keys = jax.random.split(jax.random.fold_in(key, 11), 7)
    share = 0.5
    sluggish_knots = jax.random.uniform(random_keys[0], (TRAJECTORY_COUNT, STATE_DIM)) < share
    fast_len = jax.random.uniform(random_keys[1], (TRAJECTORY_COUNT, STATE_DIM), minval=30.0, maxval=50.0)
    slow_len = 4.0 * HORIZON_KNOTS * jax.random.uniform(random_keys[2], (TRAJECTORY_COUNT, STATE_DIM), minval=1.0, maxval=3.0)
    length = jnp.where(sluggish_knots, slow_len, fast_len)
    jitter = jax.random.uniform(random_keys[3], (HORIZON_KNOTS, TRAJECTORY_COUNT, STATE_DIM), minval=0.5, maxval=1.5)
    decay_rate = jnp.exp(-jitter / length[None])
    spike_positions = jax.random.randint(random_keys[4], (3,), 0, HORIZON_KNOTS)
    knot_index = jnp.arange(HORIZON_KNOTS)
    spike_knots = jnp.any(knot_index[:, None] == spike_positions[None, :], axis=1)
    spike_multiplier = jax.random.uniform(random_keys[5], (HORIZON_KNOTS, TRAJECTORY_COUNT, STATE_DIM), minval=0.6, maxval=0.85)
    decay_rate = jnp.where(spike_knots[:, None, None] & sluggish_knots[None], decay_rate * spike_multiplier, decay_rate)
    raw = jax.random.normal(random_keys[6], (HORIZON_KNOTS, TRAJECTORY_COUNT, STATE_DIM, STATE_DIM), jnp.float32) * (0.6 / STATE_DIM ** 0.5)
    skew = 0.5 * (raw - jnp.swapaxes(raw, -1, -2))
    same = (sluggish_knots[:, :, None] == sluggish_knots[:, None, :]).astype(jnp.float32)
    skew = skew * same[None]
    eye = jnp.eye(STATE_DIM, dtype=jnp.float32)
    rotation = jnp.linalg.solve(eye + skew, jnp.broadcast_to(eye, skew.shape) - skew)
    return decay_rate[..., :, None] * rotation


def level_of(stream_key, shape, pieces, least, largest):
    factor_of, own = 1.0, jax.random.fold_in(stream_key, 6)
    for axis_at, blocks in pieces:
        draws = jnp.exp(jax.random.uniform(jax.random.fold_in(own, axis_at), (blocks,), jnp.float32, least / len(pieces), largest / len(pieces)))
        factor_of = factor_of * jnp.repeat(draws, shape[axis_at] // blocks).reshape([-1 if axis == axis_at else 1 for axis in range(len(shape))])
    return factor_of


def scatter_about(key, shape, deviation, reach, cuts=(), kind=jnp.bfloat16):
    result = deviation * jax.random.normal(key, shape, jnp.float32)
    if cuts:
        result = result * level_of(key, shape, cuts, -0.22, 0.18)
    return jnp.clip(result, -reach, reach).astype(kind)


def setup_inputs(seed: int = 0, part: int = 0) -> dict:
    seeds = jax.random.split(jax.random.key(seed), 10)
    part_keys = jax.random.split(jax.random.fold_in(seeds[9], part), 10)
    return {
        "dyn_a": draw_dyn_a(jax.random.fold_in(jax.random.fold_in(seeds[9], part), 71), part),
        "dyn_b": scatter_about(part_keys[1], (HORIZON_KNOTS, TRAJECTORY_COUNT, STATE_DIM, NU), (48 * STATE_DIM) ** -0.5, 0.109375, ((0, 16),), jnp.float32),
        "gains": scatter_about(part_keys[2], (HORIZON_KNOTS, TRAJECTORY_COUNT, NU, STATE_DIM), 0.03, 0.2, ((0, 16),), jnp.float32),
        "defects": scatter_about(part_keys[3], (HORIZON_KNOTS, TRAJECTORY_COUNT, STATE_DIM), 1.0, 6.0, ((0, 16),), jnp.float32),
        "state_grad": scatter_about(part_keys[4], (HORIZON_KNOTS, TRAJECTORY_COUNT, STATE_DIM), 1.0, 6.0, ((0, 16),), jnp.float32),
        "control_grad": scatter_about(part_keys[5], (HORIZON_KNOTS, TRAJECTORY_COUNT, NU), 0.25, 1.5, ((0, 16),), jnp.float32),
        "cost_factor": scatter_about(seeds[6], (STATE_DIM, STATE_DIM), STATE_DIM ** -0.5, 0.75, (), jnp.float32),
        "control_factor": scatter_about(seeds[7], (NU, NU), NU ** -0.5, 1.0, (), jnp.float32),
        "init_state": scatter_about(part_keys[8], (TRAJECTORY_COUNT, STATE_DIM), 1.0, 6.0, (), jnp.float32),
    }


def product(left, right):
    return jnp.matmul(left, right, precision=lax.Precision.HIGHEST)

def flipped(matrix):
    return jnp.swapaxes(matrix, -1, -2)

def apply_vec(matrix, vector):
    return product(matrix, vector[..., None])[..., 0]

def spd_solve(matrix, right_side):
    factor = jnp.linalg.cholesky(matrix)
    inner = jax.scipy.linalg.solve_triangular(factor, right_side, lower=True)
    return jax.scipy.linalg.solve_triangular(factor, inner, lower=True, trans=1)

def reference(dyn_a, dyn_b, gains, defects, state_grad, control_grad, cost_factor, control_factor, init_state):
    knots, trajs, width, controls_n = dyn_b.shape
    scale = 1.0 / math.sqrt(knots)
    term_q = jnp.eye(width, dtype=jnp.float32) + product(cost_factor, flipped(cost_factor))
    run_q = term_q / knots
    run_r = jnp.eye(controls_n, dtype=jnp.float32) + product(control_factor, flipped(control_factor))
    drift = defects * scale
    grad_q = state_grad * scale
    closed = dyn_a + product(dyn_b, gains)
    section_q = run_q + product(flipped(gains), product(run_r, gains))
    section_g = grad_q + apply_vec(flipped(gains), control_grad)

    def back_step(carry, item):
        value_mat, value_vec = carry
        a_mat, b_mat, f_mat, q_mat, d_vec, g_vec, r_vec = item
        value_b = product(value_mat, b_mat)
        hess = run_r + product(flipped(b_mat), value_b)
        cross = product(flipped(value_b), a_mat)
        lin = r_vec + apply_vec(flipped(b_mat), apply_vec(value_mat, d_vec) + value_vec)
        solved = spd_solve(hess, jnp.concatenate([cross, lin[..., None]], -1))
        new_gain = -solved[..., :width]
        feed = -solved[..., width]
        change = lax.optimization_barrier(jnp.sum(feed * lin, -1)) + 0.5 * lax.optimization_barrier(jnp.sum(feed * apply_vec(hess, feed), -1))
        next_mat = product(flipped(f_mat), product(value_mat, f_mat)) + q_mat
        next_vec = apply_vec(flipped(f_mat), value_vec + apply_vec(value_mat, d_vec)) + g_vec
        return ((next_mat, next_vec), (new_gain, feed, change))
    start = (jnp.broadcast_to(term_q, (trajs, width, width)), jnp.zeros((trajs, width), jnp.float32))
    items = (dyn_a, dyn_b, closed, section_q, drift, section_g, control_grad)
    _, (new_gains, feedforward, changes) = lax.scan(back_step, start, items, reverse=True)
    decrease = lax.optimization_barrier(jnp.sum(changes, 0)) / knots

    def forward_step(state, item):
        a_mat, b_mat, new_gain, feed, d_vec = item
        control = apply_vec(new_gain, state) + feed
        following = apply_vec(a_mat, state) + apply_vec(b_mat, control) + d_vec
        return (following, (state, control))
    _, (states, controls) = lax.scan(forward_step, init_state, (dyn_a, dyn_b, new_gains, feedforward, drift))
    return (new_gains, feedforward, states, controls, decrease)
```

```python
import functools
import math

import jax
import jax.numpy as jnp
from jax import lax
from jax.experimental import pallas as pl
from jax.experimental.pallas import tpu as pltpu
from jax.sharding import PartitionSpec as P

F32 = jnp.float32
LANES = 128
TAIL = 8


def lane_block(shape, size):
    return lax.broadcasted_iota(jnp.int32, shape, 1) // size


def spread(pair, trajs):
    block = lane_block(pair.shape, pair.shape[1] // trajs)
    return jnp.concatenate([jnp.where(block == j, pair, 0.0) for j in range(trajs)], axis=0)


def split(x):
    high = x.astype(jnp.bfloat16)
    low = (x - high.astype(F32)).astype(jnp.bfloat16)
    return high, low


def prod(left, right, flip=False):
    depth, wide = (1, 0) if flip else (0, 1)
    columns = right.shape[wide]
    if columns % LANES:
        shape = list(right.shape)
        shape[wide] = -columns % LANES
        right = jnp.concatenate([right, jnp.zeros(shape, F32)], axis=wide)
    full = right.shape[wide]
    (lh, ll), (rh, rl) = split(left), split(right)
    rows = left.shape[0]
    both = jnp.concatenate([rh, rl], axis=wide)
    dims = (((1,), (depth,)), ((), ()))
    if left.shape[1] % LANES:
        w = lax.dot_general(jnp.concatenate([lh, ll], axis=0), both, dims, preferred_element_type=F32)
        w = w[:rows] + w[rows:]
    else:
        w = lax.dot_general(
            jnp.concatenate([lh, ll], axis=1), jnp.concatenate([both, both], axis=depth), dims,
            preferred_element_type=F32,
        )
    w = w[:, :full] + w[:, full:]
    return w[:, :columns] if columns < full else w


def tail_of(row):
    shape = (TAIL, row.shape[1])
    return jnp.where(lax.broadcasted_iota(jnp.int32, shape, 0) == 0, jnp.broadcast_to(row, shape), 0.0)


def join(matrix, tail):
    return jnp.concatenate([matrix, tail], axis=0)


def apply_value(x, y, later, trajs, width):
    w = prod(later, spread(x[:width], trajs), flip=True)
    z = prod(x, spread(w[:width], trajs)) + y
    return join(z[:width], z[width:] + w[width:])


def compose_state(first, second, trajs, width):
    z = prod(first, spread(second[:width], trajs))
    return join(z[:width], z[width:] + second[width:])


def compose_value(first, second, trajs, width):
    (x1, y1), (x2, y2) = first, second
    return compose_state(x1, x2, trajs, width), apply_value(x1, y1, y2, trajs, width)


def fold(items, joined):
    while len(items) > 1:
        rest = items[len(items) // 2 * 2 :]
        items = [joined(items[i], items[i + 1]) for i in range(0, len(items) - 1, 2)] + rest
    return items[0]


def prefixes(items, joined):
    items, step = list(items), 1
    while step < len(items):
        items = [items[i] if i < step else joined(items[i - step], items[i]) for i in range(len(items))]
        step *= 2
    return items


def identity_pair(width, trajs):
    rows = lax.broadcasted_iota(jnp.int32, (width, width * trajs), 0)
    lanes = lax.broadcasted_iota(jnp.int32, (width, width * trajs), 1)
    return jnp.where(rows == lanes % width, 1.0, 0.0)


def side_by_side(rows, trajs):
    return jnp.concatenate([rows[:, j] for j in range(trajs)], axis=1)


def term_of(cost_factor, trajs):
    width = cost_factor.shape[0]
    return prod(cost_factor, jnp.concatenate([cost_factor] * trajs, axis=0), flip=True) + identity_pair(width, trajs)


def block_kernel(knots, a_ref, b_ref, g_ref, d_ref, sg_ref, cg_ref, cf_ref, rf_ref, total_ref, own_ref, term_ref):
    count, trajs, width, nu = b_ref.shape
    scale = 1.0 / math.sqrt(knots)
    term = term_of(cf_ref[...], trajs)
    run_q = term / knots
    term_ref[...] = join(term, jnp.zeros((TAIL, width * trajs), F32))
    rows = lax.broadcasted_iota(jnp.int32, (nu, nu), 0)
    lanes = lax.broadcasted_iota(jnp.int32, (nu, nu), 1)
    root = jnp.concatenate([jnp.where(rows == lanes, 1.0, 0.0), rf_ref[...]], axis=1)
    root = spread(jnp.concatenate([root] * trajs, axis=1), trajs)
    drift = side_by_side(d_ref[...], trajs) * scale
    grad = side_by_side(sg_ref[...], trajs) * scale
    cg = cg_ref[...]
    nothing = jnp.zeros((count, nu), F32)
    control = jnp.concatenate([piece for j in range(trajs) for piece in (cg[:, j], nothing)], axis=1)
    maps = []
    for t in range(count):
        at = a_ref[t].reshape(trajs * width, width).T
        bt = b_ref[t].reshape(trajs * width, nu).T
        gt = g_ref[t].reshape(trajs * nu, width).T
        both = prod(gt, jnp.concatenate([spread(bt, trajs), root], axis=1))
        x = join(at + both[:, : trajs * width], tail_of(drift[t : t + 1]))
        z = both[:, trajs * width :]
        y = prod(join(z, tail_of(control[t : t + 1])), spread(z, trajs), flip=True)
        y = y + join(run_q, tail_of(grad[t : t + 1]))
        own_ref[t, 0] = x
        own_ref[t, 1] = y
        maps.append((x, y))
    x, y = fold(maps, lambda a, b: compose_value(a, b, trajs, width))
    total_ref[0] = x
    total_ref[1] = y


def suffix_kernel(own_ref, out_ref, *, trajs, width):
    count = own_ref.shape[0]
    maps = [(own_ref[t, 0], own_ref[t, 1]) for t in reversed(range(1, count))]
    done = prefixes(maps, lambda later, earlier: compose_value(earlier, later, trajs, width))
    for i, (x, y) in enumerate(done):
        out_ref[count - 2 - i, 0] = x
        out_ref[count - 2 - i, 1] = y


def upper(step):
    return lax.rem(lax.axis_index("tm") // step, 2) == 1


def value_step_kernel(step, own_ref, got_ref, seen_ref, total_ref, next_ref, *, trajs, width):
    up = upper(step)
    own, got = (own_ref[0], own_ref[1]), (got_ref[0], got_ref[1])
    first = [jnp.where(up, g, o) for o, g in zip(own, got)]
    second = [jnp.where(up, o, g) for o, g in zip(own, got)]
    x, y = compose_value(first, second, trajs, width)
    total_ref[0] = x
    total_ref[1] = y
    if seen_ref is None:
        nothing = (join(identity_pair(width, trajs), jnp.zeros((TAIL, trajs * width), F32)), jnp.zeros_like(own[0]))
        sx, sy = got
    else:
        nothing = (seen_ref[0], seen_ref[1])
        sx, sy = compose_value(nothing, got, trajs, width)
    next_ref[0] = jnp.where(up, nothing[0], sx)
    next_ref[1] = jnp.where(up, nothing[1], sy)


def value_last_kernel(step, own_ref, got_ref, seen_ref, term_ref, value_ref, next_ref, *, trajs, width):
    up = upper(step)
    own, got = (own_ref[0], own_ref[1]), (got_ref[0], got_ref[1])
    first = [jnp.where(up, g, o) for o, g in zip(own, got)]
    second = [jnp.where(up, o, g) for o, g in zip(own, got)]
    value = apply_value(*second, term_ref[...], trajs, width)
    value_ref[...] = apply_value(*first, value, trajs, width)
    seen = (seen_ref[0], seen_ref[1])
    sx, sy = compose_value(seen, got, trajs, width)
    next_ref[0] = jnp.where(up, seen[0], sx)
    next_ref[1] = jnp.where(up, seen[1], sy)


def solve_kernel(
    knots, step, a_ref, b_ref, d_ref, cg_ref, rf_ref, term_ref, value_ref, seen_ref, suffix_ref,
    gain_ref, feed_ref, total_ref, own_ref, kt_ref,
):
    count, trajs, width, nu = b_ref.shape
    both = trajs * width
    scale = 1.0 / math.sqrt(knots)
    drift = side_by_side(d_ref[...], trajs) * scale
    control = side_by_side(cg_ref[...], trajs)
    control_columns = control.T
    rf = rf_ref[...]
    rows = lax.broadcasted_iota(jnp.int32, (nu, nu), 0)
    lanes = lax.broadcasted_iota(jnp.int32, (nu, nu), 1)
    run_r = prod(rf, rf, flip=True) + jnp.where(rows == lanes, 1.0, 0.0)
    fill = jnp.zeros((nu, both - width - nu), F32)
    run_r = jnp.concatenate([jnp.zeros((nu, width), F32), run_r, fill], axis=1)
    run_r = jnp.concatenate([run_r] * trajs, axis=0)
    lin_lane = lax.broadcasted_iota(jnp.int32, (trajs * nu, both), 1) == width + nu

    end = jnp.where(upper(step), term_ref[...], value_ref[...])
    end = apply_value(seen_ref[0], seen_ref[1], end, trajs, width)
    systems, transposed = [], []
    for t in range(count):
        value = end if t == count - 1 else apply_value(suffix_ref[t, 0], suffix_ref[t, 1], end, trajs, width)
        a = a_ref[t].reshape(both, width)
        b = b_ref[t].reshape(both, nu)
        bt = b.T
        bd = spread(bt, trajs)
        u = prod(join(bt, tail_of(drift[t : t + 1])), spread(value[:width], trajs))
        q = u[nu : nu + 1] + value[width : width + 1]
        ab = jnp.concatenate([a, b, jnp.zeros((both, both - width - nu), F32)], axis=1)
        lin = jnp.sum(bd * q, axis=1, keepdims=True) + control_columns[:, t : t + 1]
        system = prod(spread(u[:nu], trajs), ab) + run_r
        systems.append(jnp.where(lin_lane, lin, system))
        transposed.append((a.T, bd))

    solved = list(systems)
    row_at = lax.broadcasted_iota(jnp.int32, (nu, both), 0)
    for k in range(nu):
        for t in range(count):
            parts = []
            for j in range(trajs):
                s = solved[t][j * nu : (j + 1) * nu]
                pivot = s[k : k + 1]
                pivot = pivot / pivot[:, width + k : width + k + 1]
                s = s - s[:, width + k : width + k + 1] * pivot
                parts.append(jnp.where(row_at == k, pivot, s))
            solved[t] = jnp.concatenate(parts, axis=0)

    decrease = jnp.zeros((1, trajs * nu), F32)
    maps = []
    for t in range(count):
        neg = -solved[t]
        gain_ref[t] = neg[:, :width].reshape(trajs, nu, width)
        flat = neg.T
        feed = flat[width + nu : width + nu + 1]
        for j in range(trajs):
            feed_ref[t : t + 1, j] = feed[:, j * nu : (j + 1) * nu]
        kt = join(flat[:width], tail_of(feed))
        kt_ref[t] = kt
        weighted = neg[:, width + nu : width + nu + 1] * systems[t]
        parts = []
        for j in range(trajs):
            w = jnp.sum(weighted[j * nu : (j + 1) * nu], axis=0, keepdims=True)
            linear = w[:, width + nu : width + nu + 1]
            square = jnp.sum(w[:, width : width + nu] * feed[:, j * nu : (j + 1) * nu], axis=1, keepdims=True)
            parts.append(jnp.broadcast_to(linear + 0.5 * square, (1, nu)))
        decrease = decrease + jnp.concatenate(parts, axis=1)
        at, bd = transposed[t]
        m = prod(kt, bd) + join(at, tail_of(drift[t : t + 1]))
        own_ref[t] = m
        maps.append(m)
    size = width + TAIL
    total_ref[:size] = fold(maps, lambda a, b: compose_state(a, b, trajs, width))
    spare = jnp.zeros((1, both - trajs * nu), F32)
    total_ref[size:] = tail_of(jnp.concatenate([decrease, spare], axis=1))


def prefix_kernel(own_ref, out_ref, *, trajs, width):
    maps = [own_ref[t] for t in range(own_ref.shape[0] - 1)]
    for t, m in enumerate(prefixes(maps, lambda a, b: compose_state(a, b, trajs, width))):
        out_ref[t] = m


def state_step_kernel(step, own_ref, got_ref, seen_ref, total_ref, next_ref, *, trajs, width):
    up = upper(step)
    size = width + TAIL
    own, got = own_ref[:size], got_ref[:size]
    total_ref[:size] = compose_state(jnp.where(up, got, own), jnp.where(up, own, got), trajs, width)
    total_ref[size:] = own_ref[size:] + got_ref[size:]
    if seen_ref is None:
        seen = join(identity_pair(width, trajs), jnp.zeros((TAIL, trajs * width), F32))
        after = got
    else:
        seen = seen_ref[...]
        after = compose_state(got, seen, trajs, width)
    next_ref[...] = jnp.where(up, after, seen)


def state_last_kernel(step, own_ref, got_ref, seen_ref, init_ref, sent_ref, next_ref, *, trajs, width):
    up = upper(step)
    size = width + TAIL
    own, got = own_ref[:size], got_ref[:size]
    total = compose_state(jnp.where(up, got, own), jnp.where(up, own, got), trajs, width)
    init = tail_of(jnp.concatenate([init_ref[j : j + 1] for j in range(trajs)], axis=1))
    sent_ref[:TAIL] = prod(init, spread(total[:width], trajs)) + total[width:]
    sent_ref[TAIL:] = own_ref[size:] + got_ref[size:]
    seen = seen_ref[...]
    next_ref[...] = jnp.where(up, compose_state(got, seen, trajs, width), seen)


def rollout_kernel(knots, step, own_ref, got_ref, seen_ref, init_ref, prefix_ref, kt_ref,
                   state_ref, control_ref, decrease_ref):
    count, trajs, width = state_ref.shape
    nu = control_ref.shape[2]
    init = tail_of(jnp.concatenate([init_ref[j : j + 1] for j in range(trajs)], axis=1))
    start = jnp.where(upper(step), got_ref[:TAIL], init)
    start = prod(start, spread(seen_ref[:width], trajs)) + seen_ref[width:]
    for t in range(count):
        state = start
        if t > 0:
            state = prod(start, spread(prefix_ref[t - 1, :width], trajs)) + prefix_ref[t - 1, width:]
        control = prod(state, spread(kt_ref[t, :width], trajs)) + kt_ref[t, width:]
        for j in range(trajs):
            state_ref[t : t + 1, j] = state[:1, j * width : (j + 1) * width]
            control_ref[t : t + 1, j] = control[:1, j * nu : (j + 1) * nu]
    sums = (own_ref[TAIL : TAIL + 1] + got_ref[TAIL : TAIL + 1]) / knots
    for j in range(trajs):
        decrease_ref[:, j : j + 1] = sums[:, j * nu : j * nu + 1]


def call(body, outs, *args):
    return pl.pallas_call(
        body,
        out_shape=[jax.ShapeDtypeStruct(shape, F32) for shape in outs],
        compiler_params=pltpu.CompilerParams(vmem_limit_bytes=32 * 1024 * 1024),
    )(*args)


def without(body, at):
    @functools.wraps(body)
    def inner(*refs, **named):
        return body(*refs[:at], None, *refs[at:], **named)

    return inner


def shards(dyn_a, dyn_b, gains, defects, state_grad, control_grad, cost_factor, control_factor, init_state):
    count, trajs, width, nu = dyn_b.shape
    devices = lax.axis_size("tm")
    knots = count * devices
    both, size = trajs * width, width + TAIL
    sizes = dict(trajs=trajs, width=width)
    steps = [1 << i for i in range(devices.bit_length() - 1)]

    def exchange(value, step):
        return lax.ppermute(value, "tm", [(i, i ^ step) for i in range(devices)])

    total, own, term = call(
        functools.partial(block_kernel, knots),
        [(2, size, both), (count, 2, size, both), (size, both)],
        dyn_a, dyn_b, gains, defects, state_grad, control_grad, cost_factor, control_factor,
    )
    suffix, = call(functools.partial(suffix_kernel, **sizes), [(count - 1, 2, size, both)], own)
    seen = []
    for step in steps[:-2]:
        body = value_step_kernel if seen else without(value_step_kernel, 3)
        got = exchange(total, step)
        total, after = call(
            functools.partial(body, step, **sizes), [(2, size, both)] * 2, total, got, *seen
        )
        seen = [after]
    got = exchange(total, steps[-2])
    value, after = call(
        functools.partial(value_last_kernel, steps[-2], **sizes),
        [(size, both), (2, size, both)], total, got, *seen, term,
    )
    value = exchange(value, steps[-1])
    new_gains, feedforward, total, own, kt = call(
        functools.partial(solve_kernel, knots, steps[-1]),
        [(count, trajs, nu, width), (count, trajs, nu), (size + TAIL, both), (count, size, both),
         (count, size, trajs * nu)],
        dyn_a, dyn_b, defects, control_grad, control_factor, term, value, after, suffix,
    )
    prefix, = call(functools.partial(prefix_kernel, **sizes), [(count - 1, size, both)], own)
    seen = []
    for step in steps[:-2]:
        body = state_step_kernel if seen else without(state_step_kernel, 3)
        got = exchange(total, step)
        total, after = call(
            functools.partial(body, step, **sizes), [(size + TAIL, both), (size, both)], total, got, *seen
        )
        seen = [after]
    got = exchange(total, steps[-2])
    sent, after = call(
        functools.partial(state_last_kernel, steps[-2], **sizes),
        [(2 * TAIL, both), (size, both)], total, got, *seen, init_state,
    )
    got = exchange(sent, steps[-1])
    states, controls, decrease = call(
        functools.partial(rollout_kernel, knots, steps[-1]),
        [(count, trajs, width), (count, trajs, nu), (1, trajs)],
        sent, got, after, init_state, prefix, kt,
    )
    return new_gains, feedforward, states, controls, decrease.reshape(trajs)


def solution(mesh):
    in_specs = (
        P("tm", "grp", None, None),
        P("tm", "grp", None, None),
        P("tm", "grp", None, None),
        P("tm", "grp", None),
        P("tm", "grp", None),
        P("tm", "grp", None),
        P(),
        P(),
        P("grp", None),
    )
    out_specs = (
        P("tm", "grp", None, None),
        P("tm", "grp", None),
        P("tm", "grp", None),
        P("tm", "grp", None),
        P("grp"),
    )
    return jax.shard_map(shards, mesh=mesh, in_specs=in_specs, out_specs=out_specs, check_vma=False)
```

```python
import functools
import math

import jax
import jax.numpy as jnp
from jax import lax
from jax.experimental import pallas as pl
from jax.experimental.pallas import tpu as pltpu
from jax.sharding import PartitionSpec as P

F32 = jnp.float32
LANES = 128
VMEM = 60
TAIL = 8


def lane_block(shape, size):
    return lax.broadcasted_iota(jnp.int32, shape, 1) // size


def spread(pair, trajs):
    block = lane_block(pair.shape, pair.shape[1] // trajs)
    return jnp.concatenate([jnp.where(block == j, pair, 0.0) for j in range(trajs)], axis=0)


def split(x):
    high = x.astype(jnp.bfloat16)
    low = (x - high.astype(F32)).astype(jnp.bfloat16)
    return high, low


def left_of(x):
    return jnp.concatenate(split(x), axis=1)


def right_of(x, flip=False):
    depth, wide = (1, 0) if flip else (0, 1)
    both = jnp.concatenate(split(x), axis=wide)
    return jnp.concatenate([both, both], axis=depth)


def product_of(left, right, flip=False):
    dims = (((1,), (1 if flip else 0,)), ((), ()))
    w = lax.dot_general(left, right, dims, preferred_element_type=F32)
    full = w.shape[1] // 2
    return w[:, :full] + w[:, full:]


def prod(left, right, flip=False):
    wide = 0 if flip else 1
    columns = right.shape[wide]
    if columns % LANES:
        shape = list(right.shape)
        shape[wide] = -columns % LANES
        right = jnp.concatenate([right, jnp.zeros(shape, F32)], axis=wide)
    if left.shape[1] % LANES:
        rows, full = left.shape[0], right.shape[wide]
        dims = (((1,), (1 if flip else 0,)), ((), ()))
        w = lax.dot_general(
            jnp.concatenate(split(left), axis=0), jnp.concatenate(split(right), axis=wide), dims,
            preferred_element_type=F32,
        )
        w = w[:rows] + w[rows:]
        w = w[:, :full] + w[:, full:]
    else:
        w = product_of(left_of(left), right_of(right, flip), flip)
    return w[:, :columns]


def tail_of(row):
    shape = (TAIL, row.shape[1])
    return jnp.where(lax.broadcasted_iota(jnp.int32, shape, 0) == 0, jnp.broadcast_to(row, shape), 0.0)


def join(matrix, tail):
    return jnp.concatenate([matrix, tail], axis=0)


def apply_values(maps, later, trajs, width):
    ws = [prod(late, spread(x[:width], trajs), flip=True) for (x, _), late in zip(maps, later)]
    zs = [prod(x, spread(w[:width], trajs)) + y for (x, y), w in zip(maps, ws)]
    return [join(z[:width], z[width:] + w[width:]) for z, w in zip(zs, ws)]


def compose_states(pairs, trajs, width):
    zs = [prod(first, spread(second[:width], trajs)) for first, second in pairs]
    return [join(z[:width], z[width:] + second[width:]) for z, (_, second) in zip(zs, pairs)]


def compose_values(pairs, trajs, width):
    ws = [prod(second[1], spread(first[0][:width], trajs), flip=True) for first, second in pairs]
    xs = compose_states([(first[0], second[0]) for first, second in pairs], trajs, width)
    zs = [prod(first[0], spread(w[:width], trajs)) + first[1] for (first, _), w in zip(pairs, ws)]
    return [(x, join(z[:width], z[width:] + w[width:])) for x, z, w in zip(xs, zs, ws)]


def fold(items, joined):
    while len(items) > 1:
        rest = items[len(items) // 2 * 2 :]
        items = joined([(items[i], items[i + 1]) for i in range(0, len(items) - 1, 2)]) + rest
    return items[0]


def prefixes(items, joined):
    items, step = list(items), 1
    while step < len(items):
        items = items[:step] + joined([(items[i - step], items[i]) for i in range(step, len(items))])
        step *= 2
    return items


def identity_pair(width, trajs):
    rows = lax.broadcasted_iota(jnp.int32, (width, width * trajs), 0)
    lanes = lax.broadcasted_iota(jnp.int32, (width, width * trajs), 1)
    return jnp.where(rows == lanes % width, 1.0, 0.0)


def side_by_side(rows, trajs):
    return jnp.concatenate([rows[:, j] for j in range(trajs)], axis=1)


def term_of(cost_factor, trajs):
    width = cost_factor.shape[0]
    return prod(cost_factor, jnp.concatenate([cost_factor] * trajs, axis=0), flip=True) + identity_pair(width, trajs)


def paired(parts):
    return jnp.concatenate([parts[j] for j in range(parts.shape[0])], axis=1)


def block_kernel(knots, *refs):
    sources, (total_ref, *outs), held, kept, sems, out_sems = refs[:8], refs[8:13], refs[13:21], refs[21:25], *refs[25:]
    copies = [pltpu.make_async_copy(a, b, sems.at[i]) for i, (a, b) in enumerate(zip(sources, held))]
    order = (7, 2, 1, 6, 3, 4, 5, 0)
    for i in order:
        copies[i].start()
    leaving = [pltpu.make_async_copy(a, b, out_sems.at[i]) for i, (a, b) in enumerate(zip(kept, outs))]
    a_ref, bt_ref, g_ref, d_ref, sg_ref, cg_ref, cf_ref, rf_ref = held
    own_ref, term_ref, at_ref, btp_ref = kept
    count, trajs, nu, width = bt_ref.shape
    both = trajs * width
    scale = 1.0 / math.sqrt(knots)
    rows = lax.broadcasted_iota(jnp.int32, (nu, nu), 0)
    lanes = lax.broadcasted_iota(jnp.int32, (nu, nu), 1)
    for i in (7, 2, 1):
        copies[i].wait()
    root = jnp.concatenate([jnp.where(rows == lanes, 1.0, 0.0), rf_ref[...]], axis=1)
    root = spread(jnp.concatenate([root] * trajs, axis=1), trajs)
    pushed = []
    for t in range(count):
        gt = g_ref[t].reshape(trajs * nu, width).T
        btp = paired(bt_ref[t])
        btp_ref[t] = btp
        pushed.append(prod(gt, jnp.concatenate([spread(btp, trajs), root], axis=1)))
    leaving[3].start()
    for i in (6, 3, 4, 5):
        copies[i].wait()
    term = term_of(cf_ref[...], trajs)
    run_q = term / knots
    term_ref[...] = join(term, jnp.zeros((TAIL, both), F32))
    leaving[1].start()
    drift = side_by_side(d_ref[...], trajs) * scale
    grad = side_by_side(sg_ref[...], trajs) * scale
    cg = cg_ref[...]
    nothing = jnp.zeros((count, nu), F32)
    control = jnp.concatenate([piece for j in range(trajs) for piece in (cg[:, j], nothing)], axis=1)
    zs = [w[:, both:] for w in pushed]
    ys = [prod(join(z, tail_of(control[t : t + 1])), spread(z, trajs), flip=True) for t, z in enumerate(zs)]
    ys = [y + join(run_q, tail_of(grad[t : t + 1])) for t, y in enumerate(ys)]
    copies[0].wait()
    maps = []
    for t, (w, y) in enumerate(zip(pushed, ys)):
        at = a_ref[t].reshape(both, width).T
        at_ref[t] = at
        x = join(at + w[:, :both], tail_of(drift[t : t + 1]))
        own_ref[t, 0] = x
        own_ref[t, 1] = y
        maps.append((x, y))
    leaving[0].start()
    leaving[2].start()
    x, y = fold(maps, lambda pairs: compose_values(pairs, trajs, width))
    total_ref[0] = x
    total_ref[1] = y
    for copy in leaving:
        copy.wait()


def copy_kernel(source_ref, out_ref, sem):
    copy = pltpu.make_async_copy(source_ref, out_ref, sem)
    copy.start()
    copy.wait()


def suffix_kernel(own_ref, *refs, trajs, width):
    out_ref, count = refs[-1], own_ref.shape[0]
    maps = [(own_ref[t, 0], own_ref[t, 1]) for t in reversed(range(1, count))]
    done = prefixes(maps, lambda pairs: compose_values([(b, a) for a, b in pairs], trajs, width))
    for i, (x, y) in enumerate(done):
        out_ref[count - 2 - i, 0] = x
        out_ref[count - 2 - i, 1] = y


def reach_kernel(suffix_ref, seen_ref, left_ref, right_ref, y_ref, *, trajs, width):
    count = suffix_ref.shape[0] + 1
    seen = (seen_ref[0], seen_ref[1])
    maps = compose_values([((suffix_ref[t, 0], suffix_ref[t, 1]), seen) for t in range(count - 1)], trajs, width)
    for t, (x, y) in enumerate(maps + [seen]):
        left_ref[t] = left_of(join(x, jnp.zeros((left_ref.shape[1] - x.shape[0], x.shape[1]), F32)))
        right_ref[t] = right_of(spread(x[:width], trajs), flip=True)
        y_ref[t] = y


def prepare_kernel(
    knots, at_ref, btp_ref, d_ref, cg_ref, rf_ref, x_ref,
    value_ref, hess_ref, cross_ref, gain_ref, bd_ref, ad_ref, run_r_ref, control_ref, init_ref,
):
    count, nu, both = btp_ref.shape
    trajs, width = x_ref.shape
    stack = trajs * nu
    group = LANES // stack
    init_ref[...] = tail_of(jnp.concatenate([x_ref[j : j + 1] for j in range(trajs)], axis=1))
    drift = side_by_side(d_ref[...], trajs) * (1.0 / math.sqrt(knots))
    control_ref[...] = side_by_side(cg_ref[...], trajs).T
    rf = rf_ref[...]
    rows = lax.broadcasted_iota(jnp.int32, (nu, nu), 0)
    lanes = lax.broadcasted_iota(jnp.int32, (nu, nu), 1)
    run_r = prod(rf, rf, flip=True) + jnp.where(rows == lanes, 1.0, 0.0)
    run_r_ref[...] = jnp.concatenate([run_r] * (LANES // nu), axis=1)
    spare = jnp.zeros((value_ref.shape[1] - nu - TAIL, both), F32)
    bds = []
    for t in range(count):
        at, btp = at_ref[t], btp_ref[t]
        bd = spread(btp, trajs)
        bds.append(bd)
        tail = tail_of(drift[t : t + 1])
        value_ref[t] = left_of(jnp.concatenate([btp, tail, spare], axis=0))
        hess_ref[t] = right_of(
            jnp.concatenate([bd if i == t % group else jnp.zeros_like(bd) for i in range(group)], axis=0), flip=True
        )
        cross_ref[t] = right_of(jnp.concatenate([at, jnp.zeros((-width % LANES, both), F32)], axis=0), flip=True)
        bd_ref[t] = bd
        ad_ref[t] = join(at, tail)
        if len(bds) == group:
            gain_ref[t // group] = right_of(jnp.concatenate(bds, axis=0))
            bds = []


def upper(step):
    return lax.rem(lax.axis_index("tm") // step, 2) == 1


def value_step_kernel(step, own_ref, got_ref, seen_ref, *refs, trajs, width):
    total_ref, next_ref = refs[-2:]
    up = upper(step)
    own, got = (own_ref[0], own_ref[1]), (got_ref[0], got_ref[1])
    first = [jnp.where(up, g, o) for o, g in zip(own, got)]
    second = [jnp.where(up, o, g) for o, g in zip(own, got)]
    if seen_ref is None:
        seen = (join(identity_pair(width, trajs), jnp.zeros((TAIL, trajs * width), F32)), jnp.zeros_like(own[0]))
        (x, y), = compose_values([(first, second)], trajs, width)
        after = got
    else:
        seen = (seen_ref[0], seen_ref[1])
        (x, y), after = compose_values([(first, second), (seen, got)], trajs, width)
    total_ref[0] = x
    total_ref[1] = y
    next_ref[0] = jnp.where(up, seen[0], after[0])
    next_ref[1] = jnp.where(up, seen[1], after[1])


def value_last_kernel(step, own_ref, got_ref, seen_ref, term_ref, *refs, trajs, width):
    up = upper(step)
    own, got = (own_ref[0], own_ref[1]), (got_ref[0], got_ref[1])
    first = [jnp.where(up, g, o) for o, g in zip(own, got)]
    second = [jnp.where(up, o, g) for o, g in zip(own, got)]
    value_ref, next_ref = refs[-2:]
    seen, term = (seen_ref[0], seen_ref[1]), term_ref[...]
    total, (sx, sy) = compose_values([(first, second), (seen, got)], trajs, width)
    value_ref[...], = apply_values([total], [term], trajs, width)
    next_ref[0] = jnp.where(up, seen[0], sx)
    next_ref[1] = jnp.where(up, seen[1], sy)


def inverses(packs, size):
    block, step = 8, 4
    rows = lax.broadcasted_iota(jnp.int32, (block, LANES), 0)
    lanes = lax.broadcasted_iota(jnp.int32, (block, LANES), 1)
    inner = lanes % size
    first = lanes - inner
    packs = [[pack[i : i + block] for i in range(0, size, block)] for pack in packs]
    for k in range(0, size, step):
        at, r = k // block, k % block
        inside = (inner >= k) & (inner < k + step)
        for number, pack in enumerate(packs):
            columns = [[jnp.take_along_axis(x, first + (k + j), axis=1) for x in pack] for j in range(step)]
            p = [[columns[j][at][r + i : r + i + 1] for j in range(step)] for i in range(step)]
            z = [
                jnp.where(inside[:1], jnp.where(inner[:1] == k + i, 1.0, 0.0), pack[at][r + i : r + i + 1])
                for i in range(step)
            ]
            inverse = []
            for i in range(step):
                inverse.append(1.0 / p[i][i])
                for j in range(i + 1, step):
                    ratio = p[j][i] * inverse[i]
                    for c in range(i + 1, step):
                        p[j][c] = p[j][c] - ratio * p[i][c]
                    z[j] = z[j] - ratio * z[i]
            q = [None] * step
            for i in reversed(range(step)):
                v = z[i]
                for j in range(i + 1, step):
                    v = v - p[i][j] * q[j]
                q[i] = v * inverse[i]
            done = []
            for i, x in enumerate(pack):
                y = jnp.where(inside, 0.0, x)
                for j in range(step):
                    y = y - columns[j][i] * q[j]
                if i == at:
                    for j in range(step):
                        y = jnp.where(rows == r + j, q[j], y)
                done.append(y)
            packs[number] = done
    return [jnp.concatenate(pack, axis=0) for pack in packs]


def solve_kernel(
    step, term_ref, end_ref, left_ref, right_ref, y_ref,
    value_ref, hess_ref, cross_ref, gain_ref, bd_ref, ad_ref, run_r_ref, control_ref,
    total_ref, own_ref, system_ref, inverse_ref,
):
    count, stack, both = bd_ref.shape
    size = ad_ref.shape[1]
    width, nu = size - TAIL, run_r_ref.shape[0]
    trajs = both // width
    group = LANES // stack
    lin_lane = lax.broadcasted_iota(jnp.int32, (stack, LANES), 1) == width

    end = jnp.where(upper(step), term_ref[...], end_ref[...])
    end_left = left_of(end)
    ws = [product_of(end_left, right_ref[t], flip=True) for t in range(count)]
    zs = [product_of(left_ref[t], right_of(spread(w[:width], trajs)))[:size] + y_ref[t] for t, w in enumerate(ws)]
    values = [(z[:width], z[width : width + 1] + w[width : width + 1]) for z, w in zip(zs, ws)]

    us = [product_of(value_ref[t], right_of(spread(p, trajs))) for t, (p, _) in enumerate(values)]
    hesses = [product_of(left_of(u[:nu]), hess_ref[t], flip=True) for t, u in enumerate(us)]
    crosses = [product_of(left_of(spread(u[:nu], trajs)), cross_ref[t], flip=True) for t, u in enumerate(us)]
    hesses = [functools.reduce(jnp.add, hesses[t : t + group], run_r_ref[...]) for t in range(0, count, group)]
    systems, columns = [], []
    for t, (u, (_, vector)) in enumerate(zip(us, values)):
        lin = jnp.sum(bd_ref[t] * (vector + u[nu : nu + 1]), axis=1, keepdims=True) + control_ref[:, t : t + 1]
        systems.append(jnp.where(lin_lane, lin, crosses[t]))
        columns.append(lin)

    packs = inverses(hesses, nu)
    lanes = lax.broadcasted_iota(jnp.int32, (1, LANES), 1)
    flats = [jnp.concatenate(systems[t : t + group], axis=0).T[:size] for t in range(0, count, group)]
    solved = [product_of(left_of(spread(pack, LANES // nu)), gain_ref[g]) for g, pack in enumerate(packs)]
    maps = []
    for g, flat in enumerate(flats):
        left = left_of(flat)
        for i in range(group):
            mine = solved[g][i * stack : (i + 1) * stack]
            pieces = [mine if k == i else jnp.zeros_like(mine) for k in range(group)]
            maps.append(ad_ref[g * group + i] - product_of(left, right_of(jnp.concatenate(pieces, axis=0))))
    total_ref[:size] = fold(maps, lambda pairs: compose_states(pairs, trajs, width))
    for t, m in enumerate(maps):
        own_ref[t] = m

    decrease = jnp.zeros((1, LANES), F32)
    for g, (pack, flat) in enumerate(zip(packs, flats)):
        inverse_ref[g] = pack
        system_ref[g] = flat
        linear = jnp.zeros((nu, LANES), F32)
        for i in range(group):
            for j in range(trajs):
                at = i * trajs + j
                column = columns[g * group + i][j * nu : (j + 1) * nu]
                linear = jnp.where((lanes >= at * nu) & (lanes < (at + 1) * nu), column, linear)
        feed = -jnp.sum(linear * pack, axis=0, keepdims=True)
        feed_columns = jnp.broadcast_to(feed, (TAIL, LANES)).T
        weights = jnp.zeros((nu, LANES), F32)
        for at in range(LANES // nu):
            column = feed_columns[at * nu : (at + 1) * nu, :1]
            weights = jnp.where((lanes >= at * nu) & (lanes < (at + 1) * nu), column, weights)
        pushed = jnp.sum(weights * hesses[g], axis=0, keepdims=True)
        decrease = decrease + feed * flat[width : width + 1] + 0.5 * (feed * pushed)
    total_ref[size:] = tail_of(decrease)


def expand_kernel(
    own_ref, system_ref, inverse_ref, gain_ref, feed_ref, map_ref, *, trajs, width
):
    count, size, both = own_ref.shape
    groups, nu, _ = inverse_ref.shape
    group, stack = count // groups, trajs * nu
    gains = []
    kts = [-prod(system_ref[g], spread(inverse_ref[g], LANES // nu)) for g in range(groups)]
    for g, kt in enumerate(kts):
        spare = jnp.zeros((LANES - size, LANES), F32)
        natural = join(kt, spare).T
        for i in range(group):
            t = g * group + i
            gain_ref[t] = natural[i * stack : (i + 1) * stack, :width].reshape(trajs, nu, width)
            for j in range(trajs):
                at = i * stack + j * nu
                feed_ref[t : t + 1, j] = kt[width : width + 1, at : at + nu]
            gains.append(kt[:, i * stack : (i + 1) * stack])
    maps = [own_ref[t] for t in range(count - 1)]
    done = prefixes(maps, lambda pairs: compose_states(pairs, trajs, width))
    start = join(identity_pair(width, trajs), jnp.zeros((TAIL, both), F32))
    controls = [prod(m, spread(kt[:width], trajs)) for m, kt in zip(done, gains[1:])]
    controls = [join(u[:width], u[width:] + kt[width:]) for u, kt in zip(controls, gains[1:])]
    for t, (m, control) in enumerate(zip([start] + done, gains[:1] + controls)):
        map_ref[t] = jnp.concatenate([m, control, jnp.zeros((size, -stack % LANES), F32)], axis=1)


def reach_state_kernel(map_ref, seen_ref, out_ref, offset_ref, *, trajs, width, nu):
    seen = seen_ref[...]
    rows = jnp.concatenate([seen[:, j * width : (j + 1) * width] for j in range(trajs)], axis=0)
    size, both = seen.shape
    tails = map_ref[:, width:]
    products = [prod(rows, map_ref[t, :width]) for t in range(map_ref.shape[0])]
    for t, w in enumerate(products):
        lane = lax.broadcasted_iota(jnp.int32, (size, w.shape[1]), 1)
        owner = jnp.where(lane < both, lane // width, (lane - both) // nu)
        full = w[:size]
        for j in range(1, trajs):
            full = jnp.where(owner >= j, w[j * size : (j + 1) * size], full)
        out_ref[t] = jnp.concatenate(split(full[:width]), axis=1)
        offset_ref[t] = full[width:] + tails[t]


def state_step_kernel(step, own_ref, got_ref, seen_ref, total_ref, next_ref, *, trajs, width):
    up = upper(step)
    size = width + TAIL
    own, got = own_ref[:size], got_ref[:size]
    total_ref[size:] = own_ref[size:] + got_ref[size:]
    pair = (jnp.where(up, got, own), jnp.where(up, own, got))
    if seen_ref is None:
        seen = join(identity_pair(width, trajs), jnp.zeros((TAIL, trajs * width), F32))
        total_ref[:size], = compose_states([pair], trajs, width)
        after = got
    else:
        seen = seen_ref[...]
        total_ref[:size], after = compose_states([pair, (got, seen)], trajs, width)
    next_ref[...] = jnp.where(up, after, seen)


def state_last_kernel(step, own_ref, got_ref, seen_ref, init_ref, *refs, trajs, width):
    sent_ref, next_ref = refs[-2:]
    up = upper(step)
    size = width + TAIL
    own, got = own_ref[:size], got_ref[:size]
    seen = seen_ref[...]
    pair = (jnp.where(up, got, own), jnp.where(up, own, got))
    total, after = compose_states([pair, (got, seen)], trajs, width)
    sent_ref[:TAIL] = prod(init_ref[...], spread(total[:width], trajs)) + total[width:]
    sent_ref[TAIL:] = own_ref[size:] + got_ref[size:]
    next_ref[...] = jnp.where(up, after, seen)


def rows_times(row, right, trajs):
    width = right.shape[0]
    rows = jnp.concatenate([row[:1, j * width : (j + 1) * width] for j in range(trajs)], axis=0)
    left = jnp.concatenate(split(rows), axis=0)
    w = lax.dot_general(left, right, (((1,), (0,)), ((), ())), preferred_element_type=F32)
    w = w[:trajs] + w[trajs:]
    full = w.shape[1] // 2
    return w[:, :full] + w[:, full:]


def rollout_kernel(knots, step, own_ref, got_ref, init_ref, map_ref, offset_ref,
                   state_ref, control_ref, decrease_ref):
    count, trajs, width = state_ref.shape
    nu = control_ref.shape[2]
    both = trajs * width
    start = jnp.where(upper(step), got_ref[:1], init_ref[:1])
    for t in range(count):
        w = rows_times(start, map_ref[t], trajs) + offset_ref[t, :1]
        for j in range(trajs):
            state_ref[t : t + 1, j] = w[j : j + 1, j * width : (j + 1) * width]
            control_ref[t : t + 1, j] = w[j : j + 1, both + j * nu : both + (j + 1) * nu]
    sums = (own_ref[TAIL : TAIL + 1] + got_ref[TAIL : TAIL + 1]) / knots
    lane = lax.broadcasted_iota(jnp.int32, sums.shape, 1) // nu % trajs
    for j in range(trajs):
        decrease_ref[:, j : j + 1] = jnp.sum(jnp.where(lane == j, sums, 0.0), axis=1, keepdims=True)


def call(body, outs, *args, vmem=32, **named):
    return pl.pallas_call(
        body,
        out_shape=[
            jax.ShapeDtypeStruct(shape, F32) if isinstance(shape, tuple) else shape for shape in outs
        ],
        compiler_params=pltpu.CompilerParams(vmem_limit_bytes=vmem * 1024 * 1024),
        **named,
    )(*args)


def halves(*shape):
    return jax.ShapeDtypeStruct(shape, jnp.bfloat16)


def without(body, at):
    @functools.wraps(body)
    def inner(*refs, **named):
        return body(*refs[:at], None, *refs[at:], **named)

    return inner


def unread(wanted, *values):
    return values if wanted else ()


def shards(dyn_a, dyn_b, gains, defects, state_grad, control_grad, cost_factor, control_factor, init_state):
    count, trajs, width, nu = dyn_b.shape
    devices = lax.axis_size("tm")
    knots = count * devices
    both, size = trajs * width, width + TAIL
    sizes = dict(trajs=trajs, width=width)
    steps = [1 << i for i in range(devices.bit_length() - 1)]

    def exchange(value, step):
        return lax.ppermute(value, "tm", [(i, i ^ step) for i in range(devices)])

    stack = trajs * nu
    groups, up16 = count * stack // LANES, lambda n: -(-n // 16) * 16
    bt = jnp.swapaxes(dyn_b, 2, 3)
    inputs = (dyn_a, bt, gains, defects, state_grad, control_grad, cost_factor, control_factor)
    outs = [(2, size, both), (count, 2, size, both), (size, both), (count, width, both), (count, nu, both)]
    total, own, term, at, btp = call(
        functools.partial(block_kernel, knots), outs, *inputs,
        vmem=VMEM,
        in_specs=[pl.BlockSpec(memory_space=pl.ANY)] * len(inputs),
        out_specs=[pl.BlockSpec(memory_space=pltpu.VMEM)] + [pl.BlockSpec(memory_space=pl.ANY)] * 4,
        scratch_shapes=[pltpu.VMEM(x.shape, F32) for x in inputs] + [pltpu.VMEM(shape, F32) for shape in outs[1:]]
        + [pltpu.SemaphoreType.DMA((len(inputs),)), pltpu.SemaphoreType.DMA((4,))],
    )
    suffix, = call(functools.partial(suffix_kernel, **sizes), [(count - 1, 2, size, both)], own)
    *ready, init = call(
        functools.partial(prepare_kernel, knots),
        [halves(count, up16(nu + TAIL), 2 * both), halves(count, 2 * LANES, 2 * both),
         halves(count, 2 * LANES, 2 * both), halves(groups, 2 * LANES, 2 * both), (count, stack, both),
         (count, size, both), (nu, LANES), (stack, count), (TAIL, both)],
        at, btp, defects, control_grad, control_factor, init_state,
    )
    got = exchange(total, steps[0])
    total, = call(
        copy_kernel, [(2, size, both)], total,
        in_specs=[pl.BlockSpec(memory_space=pl.ANY)], scratch_shapes=[pltpu.SemaphoreType.DMA],
    )
    total, after = call(
        functools.partial(without(value_step_kernel, 3), steps[0], **sizes), [(2, size, both)] * 2, total, got
    )
    for i, step in enumerate(steps[1:-2]):
        got = exchange(total, step)
        total, after = call(
            functools.partial(value_step_kernel, step, **sizes), [(2, size, both)] * 2,
            total, got, after, *unread(i == 0, init),
        )
    got = exchange(total, steps[-2])
    value, after = call(
        functools.partial(value_last_kernel, steps[-2], **sizes),
        [(size, both), (2, size, both)], total, got, after, term, suffix,
    )
    reach = call(
        functools.partial(reach_kernel, **sizes),
        [halves(count, up16(size), 2 * both), halves(count, 2 * both, 2 * both), (count, size, both)], suffix, after,
    )
    value = exchange(value, steps[-1])
    total, own, system, inverse = call(
        functools.partial(solve_kernel, steps[-1]),
        [(size + TAIL, both), (count, size, both), (groups, size, LANES), (groups, nu, LANES)],
        term, value, *reach, *ready,
    )
    wide = both + -(-stack // LANES) * LANES
    new_gains, feedforward, maps = call(
        functools.partial(expand_kernel, **sizes),
        [(count, trajs, nu, width), (count, trajs, nu), (count, size, wide)], own, system, inverse,
    )
    seen = []
    for step in steps[:-2]:
        body = state_step_kernel if seen else without(state_step_kernel, 3)
        got = exchange(total, step)
        total, after = call(
            functools.partial(body, step, **sizes), [(size + TAIL, both), (size, both)], total, got, *seen
        )
        seen = [after]
    got = exchange(total, steps[-2])
    sent, after = call(
        functools.partial(state_last_kernel, steps[-2], **sizes),
        [(2 * TAIL, both), (size, both)], total, got, *seen, init, maps,
    )
    maps, offsets = call(
        functools.partial(reach_state_kernel, **sizes, nu=nu),
        [halves(count, width, 2 * wide), (count, TAIL, wide)], maps, after,
    )
    got = exchange(sent, steps[-1])
    states, controls, decrease = call(
        functools.partial(rollout_kernel, knots, steps[-1]),
        [(count, trajs, width), (count, trajs, nu), (1, trajs)],
        sent, got, init, maps, offsets,
    )
    return new_gains, feedforward, states, controls, decrease.reshape(trajs)


def solution(mesh):
    in_specs = (
        P("tm", "grp", None, None),
        P("tm", "grp", None, None),
        P("tm", "grp", None, None),
        P("tm", "grp", None),
        P("tm", "grp", None),
        P("tm", "grp", None),
        P(),
        P(),
        P("grp", None),
    )
    out_specs = (
        P("tm", "grp", None, None),
        P("tm", "grp", None),
        P("tm", "grp", None),
        P("tm", "grp", None),
        P("grp"),
    )
    return jax.shard_map(shards, mesh=mesh, in_specs=in_specs, out_specs=out_specs, check_vma=False)
```

```python
import functools
import math

import jax
import jax.numpy as jnp
from jax import lax
from jax.experimental import pallas as pl
from jax.experimental.pallas import tpu as pltpu
from jax.sharding import PartitionSpec as P

F32 = jnp.float32
LANES = 128
TAIL = 8


def lane_block(shape, size):
    return lax.broadcasted_iota(jnp.int32, shape, 1) // size


def spread(pair, trajs):
    block = lane_block(pair.shape, pair.shape[1] // trajs)
    return jnp.concatenate([jnp.where(block == j, pair, 0.0) for j in range(trajs)], axis=0)


def split(x):
    high = x.astype(jnp.bfloat16)
    low = (x - high.astype(F32)).astype(jnp.bfloat16)
    return high, low


def left_of(x):
    return jnp.concatenate(split(x), axis=1)


def right_of(x, flip=False):
    depth, wide = (1, 0) if flip else (0, 1)
    both = jnp.concatenate(split(x), axis=wide)
    return jnp.concatenate([both, both], axis=depth)


def product_of(left, right, flip=False):
    dims = (((1,), (1 if flip else 0,)), ((), ()))
    w = lax.dot_general(left, right, dims, preferred_element_type=F32)
    full = w.shape[1] // 2
    return w[:, :full] + w[:, full:]


def prod(left, right, flip=False):
    wide = 0 if flip else 1
    columns = right.shape[wide]
    if columns % LANES:
        shape = list(right.shape)
        shape[wide] = -columns % LANES
        right = jnp.concatenate([right, jnp.zeros(shape, F32)], axis=wide)
    if left.shape[1] % LANES:
        rows, full = left.shape[0], right.shape[wide]
        dims = (((1,), (1 if flip else 0,)), ((), ()))
        w = lax.dot_general(
            jnp.concatenate(split(left), axis=0), jnp.concatenate(split(right), axis=wide), dims,
            preferred_element_type=F32,
        )
        w = w[:rows] + w[rows:]
        w = w[:, :full] + w[:, full:]
    else:
        w = product_of(left_of(left), right_of(right, flip), flip)
    return w[:, :columns]


def tail_of(row):
    shape = (TAIL, row.shape[1])
    return jnp.where(lax.broadcasted_iota(jnp.int32, shape, 0) == 0, jnp.broadcast_to(row, shape), 0.0)


def join(matrix, tail):
    return jnp.concatenate([matrix, tail], axis=0)


def apply_values(maps, later, trajs, width):
    ws = [prod(late, spread(x[:width], trajs), flip=True) for (x, _), late in zip(maps, later)]
    zs = [prod(x, spread(w[:width], trajs)) + y for (x, y), w in zip(maps, ws)]
    return [join(z[:width], z[width:] + w[width:]) for z, w in zip(zs, ws)]


def compose_states(pairs, trajs, width):
    zs = [prod(first, spread(second[:width], trajs)) for first, second in pairs]
    return [join(z[:width], z[width:] + second[width:]) for z, (_, second) in zip(zs, pairs)]


def compose_values(pairs, trajs, width):
    ws = [prod(second[1], spread(first[0][:width], trajs), flip=True) for first, second in pairs]
    xs = compose_states([(first[0], second[0]) for first, second in pairs], trajs, width)
    zs = [prod(first[0], spread(w[:width], trajs)) + first[1] for (first, _), w in zip(pairs, ws)]
    return [(x, join(z[:width], z[width:] + w[width:])) for x, z, w in zip(xs, zs, ws)]


def fold(items, joined):
    while len(items) > 1:
        rest = items[len(items) // 2 * 2 :]
        items = joined([(items[i], items[i + 1]) for i in range(0, len(items) - 1, 2)]) + rest
    return items[0]


def prefixes(items, joined):
    items, step = list(items), 1
    while step < len(items):
        late = [i for i in range(len(items)) if i // step % 2]
        for i, joint in zip(late, joined([(items[i // step * step - 1], items[i]) for i in late])):
            items[i] = joint
        step *= 2
    return items


def identity_pair(width, trajs):
    rows = lax.broadcasted_iota(jnp.int32, (width, width * trajs), 0)
    lanes = lax.broadcasted_iota(jnp.int32, (width, width * trajs), 1)
    return jnp.where(rows == lanes % width, 1.0, 0.0)


def side_by_side(rows, trajs):
    return jnp.concatenate([rows[:, j] for j in range(trajs)], axis=1)


def term_of(cost_factor, trajs):
    width = cost_factor.shape[0]
    return prod(cost_factor, jnp.concatenate([cost_factor] * trajs, axis=0), flip=True) + identity_pair(width, trajs)


def paired(parts):
    return jnp.concatenate([parts[j] for j in range(parts.shape[0])], axis=1)


def block_kernel(knots, *refs):
    sources, (total_ref, own_ref, term_ref, at_ref, btp_ref), held, sems = refs[:8], refs[8:13], refs[13:21], refs[21]
    copies = [pltpu.make_async_copy(a, b, sems.at[i]) for i, (a, b) in enumerate(zip(sources, held))]
    order = (7, 2, 1, 6, 3, 4, 5, 0)
    for i in order:
        copies[i].start()
    a_ref, bt_ref, g_ref, d_ref, sg_ref, cg_ref, cf_ref, rf_ref = held
    count, trajs, nu, width = bt_ref.shape
    both = trajs * width
    scale = 1.0 / math.sqrt(knots)
    rows = lax.broadcasted_iota(jnp.int32, (nu, nu), 0)
    lanes = lax.broadcasted_iota(jnp.int32, (nu, nu), 1)
    for i in (7, 2, 1):
        copies[i].wait()
    root = jnp.concatenate([jnp.where(rows == lanes, 1.0, 0.0), rf_ref[...]], axis=1)
    root = spread(jnp.concatenate([root] * trajs, axis=1), trajs)
    pushed = []
    for t in range(count):
        gt = g_ref[t].reshape(trajs * nu, width).T
        btp = paired(bt_ref[t])
        btp_ref[t] = btp
        pushed.append(prod(gt, jnp.concatenate([spread(btp, trajs), root], axis=1)))
    for i in (6, 3, 4, 5):
        copies[i].wait()
    term = term_of(cf_ref[...], trajs)
    run_q = term / knots
    term_ref[...] = join(term, jnp.zeros((TAIL, both), F32))
    drift = side_by_side(d_ref[...], trajs) * scale
    grad = side_by_side(sg_ref[...], trajs) * scale
    cg = cg_ref[...]
    nothing = jnp.zeros((count, nu), F32)
    control = jnp.concatenate([piece for j in range(trajs) for piece in (cg[:, j], nothing)], axis=1)
    zs = [w[:, both:] for w in pushed]
    ys = [prod(join(z, tail_of(control[t : t + 1])), spread(z, trajs), flip=True) for t, z in enumerate(zs)]
    ys = [y + join(run_q, tail_of(grad[t : t + 1])) for t, y in enumerate(ys)]
    copies[0].wait()
    maps = []
    for t, (w, y) in enumerate(zip(pushed, ys)):
        at = a_ref[t].reshape(both, width).T
        at_ref[t] = at
        x = join(at + w[:, :both], tail_of(drift[t : t + 1]))
        own_ref[t, 0] = x
        own_ref[t, 1] = y
        maps.append((x, y))
    befores = prefixes([x for x, _ in maps], lambda pairs: compose_states(pairs, trajs, width))
    nothing = jnp.zeros_like(maps[0][1])
    parts = apply_values([(x, nothing) for x in befores[:-1]], [y for _, y in maps[1:]], trajs, width)
    total_ref[0] = befores[-1]
    total_ref[1] = functools.reduce(jnp.add, parts, maps[0][1])


def suffix_kernel(own_ref, *refs, trajs, width):
    out_ref, count = refs[-1], own_ref.shape[0]
    maps = [(own_ref[t, 0], own_ref[t, 1]) for t in reversed(range(1, count))]
    done = prefixes(maps, lambda pairs: compose_values([(b, a) for a, b in pairs], trajs, width))
    for i, (x, y) in enumerate(done):
        out_ref[count - 2 - i, 0] = x
        out_ref[count - 2 - i, 1] = y


def prepare_kernel(
    knots, at_ref, btp_ref, d_ref, cg_ref, rf_ref, x_ref,
    left_ref, hess_ref, cross_ref, gain_ref, bd_ref, ad_ref, run_r_ref, control_ref, init_ref,
):
    count, nu, both = btp_ref.shape
    trajs, width = x_ref.shape
    stack = trajs * nu
    group = LANES // stack
    init_ref[...] = tail_of(jnp.concatenate([x_ref[j : j + 1] for j in range(trajs)], axis=1))
    drift = side_by_side(d_ref[...], trajs) * (1.0 / math.sqrt(knots))
    control_ref[...] = side_by_side(cg_ref[...], trajs).T
    rf = rf_ref[...]
    rows = lax.broadcasted_iota(jnp.int32, (nu, nu), 0)
    lanes = lax.broadcasted_iota(jnp.int32, (nu, nu), 1)
    run_r = prod(rf, rf, flip=True) + jnp.where(rows == lanes, 1.0, 0.0)
    run_r_ref[...] = jnp.concatenate([run_r] * (LANES // nu), axis=1)
    spare = jnp.zeros((left_ref.shape[1] - nu - TAIL - width, both), F32)
    bds = []
    for t in range(count):
        at, btp = at_ref[t], btp_ref[t]
        bd = spread(btp, trajs)
        bds.append(bd)
        tail = tail_of(drift[t : t + 1])
        left_ref[t] = left_of(jnp.concatenate([btp, tail, at, spare], axis=0))
        hess_ref[t] = placed(bd, t % group, group)
        cross_ref[t] = right_of(over(at), flip=True)
        bd_ref[t] = bd
        ad_ref[t] = join(at, tail)
        if len(bds) == group:
            gain_ref[t // group] = right_of(jnp.concatenate(bds, axis=0))
            bds = []


def placed(bd, at, group):
    return right_of(jnp.concatenate([bd if i == at else jnp.zeros_like(bd) for i in range(group)], axis=0), flip=True)


def over(matrix):
    return jnp.concatenate([matrix, jnp.zeros((-matrix.shape[0] % LANES, matrix.shape[1]), F32)], axis=0)


def reach_kernel(
    suffix_ref, seen_ref, left_ref, hess_ref, cross_ref, bd_ref, run_r_ref, control_ref,
    value_out, hess_out, cross_out, bd_out, hess_base, cross_base, *, trajs, width,
):
    count, nu = left_ref.shape[0], run_r_ref.shape[0]
    group = count // hess_base.shape[0]
    seen = (seen_ref[0], seen_ref[1])
    maps = compose_values([((suffix_ref[t, 0], suffix_ref[t, 1]), seen) for t in range(count - 1)], trajs, width)
    maps.append(seen)
    both = trajs * width
    rows = value_out.shape[1]
    firsts = [product_of(left_ref[t], right_of(spread(x[:width], trajs))) for t, (x, _) in enumerate(maps)]
    us = [product_of(left_ref[t, :rows], right_of(spread(y[:width], trajs))) for t, (_, y) in enumerate(maps)]
    hesses = [product_of(left_of(u[:nu]), hess_ref[t], flip=True) for t, u in enumerate(us)]
    crosses = [product_of(left_of(spread(u[:nu], trajs)), cross_ref[t], flip=True) for t, u in enumerate(us)]
    lin_lane = lax.broadcasted_iota(jnp.int32, crosses[0].shape, 1) == width
    spare = jnp.zeros((rows - nu - TAIL, both), F32)
    for t, (w, (x, y)) in enumerate(zip(firsts, maps)):
        bd = spread(w[:nu], trajs)
        value_out[t] = left_of(jnp.concatenate([w[:nu], w[nu : nu + TAIL] + x[width:], spare], axis=0))
        hess_out[t] = placed(bd, t % group, group)
        cross_out[t] = right_of(over(w[nu + TAIL : nu + TAIL + width]), flip=True)
        bd_out[t] = bd
        vector = us[t][nu : nu + 1] + y[width : width + 1]
        lin = jnp.sum(bd_ref[t] * vector, axis=1, keepdims=True) + control_ref[:, t : t + 1]
        cross_base[t] = jnp.where(lin_lane, lin, crosses[t])
    for g in range(count // group):
        hess_base[g] = functools.reduce(jnp.add, hesses[g * group : (g + 1) * group], run_r_ref[...])


def upper(step):
    return lax.rem(lax.axis_index("tm") // step, 2) == 1


def value_step_kernel(step, own_ref, got_ref, seen_ref, *refs, trajs, width):
    total_ref, next_ref = refs[-2:]
    up = upper(step)
    own, got = (own_ref[0], own_ref[1]), (got_ref[0], got_ref[1])
    first = [jnp.where(up, g, o) for o, g in zip(own, got)]
    second = [jnp.where(up, o, g) for o, g in zip(own, got)]
    if seen_ref is None:
        seen = (join(identity_pair(width, trajs), jnp.zeros((TAIL, trajs * width), F32)), jnp.zeros_like(own[0]))
        (x, y), = compose_values([(first, second)], trajs, width)
        after = got
    else:
        seen = (seen_ref[0], seen_ref[1])
        (x, y), after = compose_values([(first, second), (seen, got)], trajs, width)
    total_ref[0] = x
    total_ref[1] = y
    next_ref[0] = jnp.where(up, seen[0], after[0])
    next_ref[1] = jnp.where(up, seen[1], after[1])


def value_last_kernel(step, own_ref, got_ref, seen_ref, term_ref, *refs, trajs, width):
    up = upper(step)
    own, got = (own_ref[0], own_ref[1]), (got_ref[0], got_ref[1])
    first = [jnp.where(up, g, o) for o, g in zip(own, got)]
    second = [jnp.where(up, o, g) for o, g in zip(own, got)]
    value_ref, next_ref = refs[-2:]
    seen, term = (seen_ref[0], seen_ref[1]), term_ref[...]
    total, (sx, sy) = compose_values([(first, second), (seen, got)], trajs, width)
    value_ref[...], = apply_values([total], [term], trajs, width)
    next_ref[0] = jnp.where(up, seen[0], sx)
    next_ref[1] = jnp.where(up, seen[1], sy)


def factors(packs, size):
    block, step = 8, 4
    rows = lax.broadcasted_iota(jnp.int32, (block, LANES), 0)
    lanes = lax.broadcasted_iota(jnp.int32, (block, LANES), 1)
    inner = lanes % size
    first = lanes - inner
    packs = [[pack[i : i + block] for i in range(0, size, block)] for pack in packs]
    ws = [[jnp.zeros((block, LANES), F32) for _ in pack] for pack in packs]
    qs = [list(w) for w in ws]
    for k in range(0, size, step):
        at, r = k // block, k % block
        inside = (inner >= k) & (inner < k + step)
        known = inner[:1] < k + step
        for number, pack in enumerate(packs):
            columns = {
                i: [jnp.take_along_axis(pack[i], first + (k + j), axis=1) for j in range(step)]
                for i in range(at, len(pack))
            }
            p = [[columns[at][j][r + i : r + i + 1] for j in range(step)] for i in range(step)]
            z = [
                jnp.where(inside[:1], jnp.where(inner[:1] == k + i, 1.0, 0.0), pack[at][r + i : r + i + 1])
                for i in range(step)
            ]
            for i in range(step):
                ws[number][at] = jnp.where(rows == r + i, jnp.where(known, z[i], 0.0), ws[number][at])
            inverse = []
            for i in range(step):
                inverse.append(1.0 / p[i][i])
                for j in range(i + 1, step):
                    ratio = p[j][i] * inverse[i]
                    for c in range(i + 1, step):
                        p[j][c] = p[j][c] - ratio * p[i][c]
                    z[j] = z[j] - ratio * z[i]
            q = [None] * step
            for i in reversed(range(step)):
                v = z[i]
                for j in range(i + 1, step):
                    v = v - p[i][j] * q[j]
                q[i] = v * inverse[i]
            for i in range(step):
                qs[number][at] = jnp.where(rows == r + i, jnp.where(known, q[i], 0.0), qs[number][at])
            for i in range(at if r + step < block else at + 1, len(pack)):
                y = jnp.where(inside, 0.0, pack[i])
                for j in range(step):
                    y = y - columns[i][j] * q[j]
                pack[i] = y
    return [(jnp.concatenate(w, axis=0), jnp.concatenate(q, axis=0)) for w, q in zip(ws, qs)]


def solve_kernel(
    step, term_ref, end_ref, value_ref, hess_ref, cross_ref, bd_ref, hess_base, cross_base, gain_ref, ad_ref,
    total_ref, own_ref, half_ref, q_ref,
):
    count, stack, both = bd_ref.shape
    size = ad_ref.shape[1]
    groups, nu, _ = hess_base.shape
    width = size - TAIL
    trajs, group = both // width, count // groups
    rows = value_ref.shape[1]
    lin_lane = lax.broadcasted_iota(jnp.int32, (stack, LANES), 1) == width

    end = jnp.where(upper(step), term_ref[...], end_ref[...])
    w = product_of(value_ref[...].reshape(count * rows, 2 * both), right_of(spread(end[:width], trajs)))
    us = [w[t * rows : t * rows + nu] for t in range(count)]
    hesses = [product_of(left_of(u), hess_ref[t], flip=True) for t, u in enumerate(us)]
    hesses = [functools.reduce(jnp.add, hesses[g * group : (g + 1) * group], hess_base[g]) for g in range(groups)]
    pairs = factors(hesses, nu)
    crosses = [product_of(left_of(spread(u, trajs)), cross_ref[t], flip=True) for t, u in enumerate(us)]
    systems = []
    for t, cross in enumerate(crosses):
        vector = w[t * rows + nu : t * rows + nu + 1] + end[width : width + 1]
        lin = jnp.sum(bd_ref[t] * vector, axis=1, keepdims=True)
        systems.append(jnp.where(lin_lane, lin, cross) + cross_base[t])

    flats = [jnp.concatenate(systems[t : t + group], axis=0).T[:size] for t in range(0, count, group)]
    lefts = [left_of(flat) for flat in flats]
    lanes = lax.broadcasted_iota(jnp.int32, (1, LANES), 1)
    spreads = [(spread(w, LANES // nu), spread(q, LANES // nu)) for w, q in pairs]
    halves = [product_of(left, right_of(w, flip=True), flip=True) for left, (w, _) in zip(lefts, spreads)]
    pushes = [product_of(left_of(q), gain_ref[g]) for g, (_, q) in enumerate(spreads)]
    maps = []
    for g, half in enumerate(halves):
        left = left_of(half)
        for i in range(group):
            mine = pushes[g][i * stack : (i + 1) * stack]
            pieces = [mine if k == i else jnp.zeros_like(mine) for k in range(group)]
            maps.append(ad_ref[g * group + i] - product_of(left, right_of(jnp.concatenate(pieces, axis=0))))
    total_ref[:size] = fold(maps, lambda pairs: compose_states(pairs, trajs, width))
    for t, m in enumerate(maps):
        own_ref[t] = m

    decrease = jnp.zeros((1, LANES), F32)
    for g, (half, flat) in enumerate(zip(halves, flats)):
        half_ref[g] = half
        q_ref[g] = pairs[g][1]
        feed = -prod(half[width:], spreads[g][1])[:1]
        feed_columns = jnp.broadcast_to(feed, (TAIL, LANES)).T
        weights = jnp.zeros((nu, LANES), F32)
        for at in range(LANES // nu):
            column = feed_columns[at * nu : (at + 1) * nu, :1]
            weights = jnp.where((lanes >= at * nu) & (lanes < (at + 1) * nu), column, weights)
        pushed = jnp.sum(weights * hesses[g], axis=0, keepdims=True)
        decrease = decrease + feed * flat[width : width + 1] + 0.5 * (feed * pushed)
    total_ref[size:] = tail_of(decrease)


def expand_kernel(
    own_ref, half_ref, q_ref, gain_ref, feed_ref, map_ref, *, trajs, width
):
    count, size, both = own_ref.shape
    groups, nu, _ = q_ref.shape
    group, stack = count // groups, trajs * nu
    gains = []
    kts = [-prod(half_ref[g], spread(q_ref[g], LANES // nu)) for g in range(groups)]
    for g, kt in enumerate(kts):
        spare = jnp.zeros((LANES - size, LANES), F32)
        natural = join(kt, spare).T
        for i in range(group):
            t = g * group + i
            gain_ref[t] = natural[i * stack : (i + 1) * stack, :width].reshape(trajs, nu, width)
            for j in range(trajs):
                at = i * stack + j * nu
                feed_ref[t : t + 1, j] = kt[width : width + 1, at : at + nu]
            gains.append(kt[:, i * stack : (i + 1) * stack])
    maps = [own_ref[t] for t in range(count - 1)]
    done = prefixes(maps, lambda pairs: compose_states(pairs, trajs, width))
    start = join(identity_pair(width, trajs), jnp.zeros((TAIL, both), F32))
    controls = [prod(m, spread(kt[:width], trajs)) for m, kt in zip(done, gains[1:])]
    controls = [join(u[:width], u[width:] + kt[width:]) for u, kt in zip(controls, gains[1:])]
    for t, (m, control) in enumerate(zip([start] + done, gains[:1] + controls)):
        map_ref[t] = jnp.concatenate([m, control, jnp.zeros((size, -stack % LANES), F32)], axis=1)


def reach_state_kernel(map_ref, seen_ref, out_ref, offset_ref, *, trajs, width, nu):
    seen = seen_ref[...]
    rows = jnp.concatenate([seen[:, j * width : (j + 1) * width] for j in range(trajs)], axis=0)
    size, both = seen.shape
    tails = map_ref[:, width:]
    products = [prod(rows, map_ref[t, :width]) for t in range(map_ref.shape[0])]
    for t, w in enumerate(products):
        lane = lax.broadcasted_iota(jnp.int32, (size, w.shape[1]), 1)
        owner = jnp.where(lane < both, lane // width, (lane - both) // nu)
        full = w[:size]
        for j in range(1, trajs):
            full = jnp.where(owner >= j, w[j * size : (j + 1) * size], full)
        out_ref[t] = jnp.concatenate(split(full[:width]), axis=1)
        offset_ref[t] = full[width:] + tails[t]


def state_step_kernel(step, own_ref, got_ref, seen_ref, total_ref, next_ref, *, trajs, width):
    up = upper(step)
    size = width + TAIL
    own, got = own_ref[:size], got_ref[:size]
    total_ref[size:] = own_ref[size:] + got_ref[size:]
    pair = (jnp.where(up, got, own), jnp.where(up, own, got))
    if seen_ref is None:
        seen = join(identity_pair(width, trajs), jnp.zeros((TAIL, trajs * width), F32))
        total_ref[:size], = compose_states([pair], trajs, width)
        after = got
    else:
        seen = seen_ref[...]
        total_ref[:size], after = compose_states([pair, (got, seen)], trajs, width)
    next_ref[...] = jnp.where(up, after, seen)


def state_last_kernel(step, own_ref, got_ref, seen_ref, init_ref, *refs, trajs, width):
    sent_ref, next_ref = refs[-2:]
    up = upper(step)
    size = width + TAIL
    own, got = own_ref[:size], got_ref[:size]
    seen = seen_ref[...]
    pair = (jnp.where(up, got, own), jnp.where(up, own, got))
    total, after = compose_states([pair, (got, seen)], trajs, width)
    sent_ref[:TAIL] = prod(init_ref[...], spread(total[:width], trajs)) + total[width:]
    sent_ref[TAIL:] = own_ref[size:] + got_ref[size:]
    next_ref[...] = jnp.where(up, after, seen)


def rows_times(row, right, trajs):
    width = right.shape[0]
    rows = jnp.concatenate([row[:1, j * width : (j + 1) * width] for j in range(trajs)], axis=0)
    left = jnp.concatenate(split(rows), axis=0)
    w = lax.dot_general(left, right, (((1,), (0,)), ((), ())), preferred_element_type=F32)
    w = w[:trajs] + w[trajs:]
    full = w.shape[1] // 2
    return w[:, :full] + w[:, full:]


def rollout_kernel(knots, step, own_ref, got_ref, init_ref, map_ref, offset_ref,
                   state_ref, control_ref, decrease_ref):
    count, trajs, width = state_ref.shape
    nu = control_ref.shape[2]
    both = trajs * width
    start = jnp.where(upper(step), got_ref[:1], init_ref[:1])
    for t in range(count):
        w = rows_times(start, map_ref[t], trajs) + offset_ref[t, :1]
        for j in range(trajs):
            state_ref[t : t + 1, j] = w[j : j + 1, j * width : (j + 1) * width]
            control_ref[t : t + 1, j] = w[j : j + 1, both + j * nu : both + (j + 1) * nu]
    sums = (own_ref[TAIL : TAIL + 1] + got_ref[TAIL : TAIL + 1]) / knots
    lane = lax.broadcasted_iota(jnp.int32, sums.shape, 1) // nu % trajs
    for j in range(trajs):
        decrease_ref[:, j : j + 1] = jnp.sum(jnp.where(lane == j, sums, 0.0), axis=1, keepdims=True)


def call(body, outs, *args, **named):
    return pl.pallas_call(
        body,
        out_shape=[
            jax.ShapeDtypeStruct(shape, F32) if isinstance(shape, tuple) else shape for shape in outs
        ],
        compiler_params=pltpu.CompilerParams(vmem_limit_bytes=32 * 1024 * 1024),
        **named,
    )(*args)


def halves(*shape):
    return jax.ShapeDtypeStruct(shape, jnp.bfloat16)


def without(body, at):
    @functools.wraps(body)
    def inner(*refs, **named):
        return body(*refs[:at], None, *refs[at:], **named)

    return inner


def unread(wanted, *values):
    return values if wanted else ()


def shards(dyn_a, dyn_b, gains, defects, state_grad, control_grad, cost_factor, control_factor, init_state):
    count, trajs, width, nu = dyn_b.shape
    devices = lax.axis_size("tm")
    knots = count * devices
    both, size = trajs * width, width + TAIL
    sizes = dict(trajs=trajs, width=width)
    steps = [1 << i for i in range(devices.bit_length() - 1)]

    def exchange(value, step):
        return lax.ppermute(value, "tm", [(i, i ^ step) for i in range(devices)])

    stack = trajs * nu
    groups, up16 = count * stack // LANES, lambda n: -(-n // 16) * 16
    bt = jnp.swapaxes(dyn_b, 2, 3)
    inputs = (dyn_a, bt, gains, defects, state_grad, control_grad, cost_factor, control_factor)
    total, own, term, at, btp = call(
        functools.partial(block_kernel, knots),
        [(2, size, both), (count, 2, size, both), (size, both), (count, width, both), (count, nu, both)],
        *[pltpu.with_memory_space_constraint(x, pltpu.HBM) for x in inputs],
        in_specs=[pl.BlockSpec(memory_space=pltpu.HBM)] * len(inputs),
        scratch_shapes=[pltpu.VMEM(x.shape, F32) for x in inputs] + [pltpu.SemaphoreType.DMA((len(inputs),))],
    )
    suffix, = call(functools.partial(suffix_kernel, **sizes), [(count - 1, 2, size, both)], own)
    turned = (count, 2 * LANES, 2 * both)
    left, hess, cross, gain, bd, ad, run_r, control, init = call(
        functools.partial(prepare_kernel, knots),
        [halves(count, up16(nu + TAIL + width), 2 * both), halves(*turned), halves(*turned),
         halves(groups, *turned[1:]), (count, stack, both), (count, size, both), (nu, LANES), (stack, count),
         (TAIL, both)],
        at, btp, defects, control_grad, control_factor, init_state,
    )
    got = exchange(total, steps[0])
    total, after = call(
        functools.partial(without(value_step_kernel, 3), steps[0], **sizes), [(2, size, both)] * 2, total, got
    )
    for i, step in enumerate(steps[1:-2]):
        got = exchange(total, step)
        total, after = call(
            functools.partial(value_step_kernel, step, **sizes), [(2, size, both)] * 2,
            total, got, after, *unread(i == 0, init),
        )
    got = exchange(total, steps[-2])
    value, after = call(
        functools.partial(value_last_kernel, steps[-2], **sizes),
        [(size, both), (2, size, both)], total, got, after, term, suffix,
    )
    reach = call(
        functools.partial(reach_kernel, **sizes),
        [halves(count, up16(nu + TAIL), 2 * both), halves(*turned), halves(*turned), (count, stack, both),
         (groups, nu, LANES), (count, stack, LANES)],
        suffix, after, left, hess, cross, bd, run_r, control,
    )
    value = exchange(value, steps[-1])
    total, own, half, q = call(
        functools.partial(solve_kernel, steps[-1]),
        [(size + TAIL, both), (count, size, both), (groups, size, LANES), (groups, nu, LANES)],
        term, value, *reach, gain, ad,
    )
    wide = both + -(-stack // LANES) * LANES
    new_gains, feedforward, maps = call(
        functools.partial(expand_kernel, **sizes),
        [(count, trajs, nu, width), (count, trajs, nu), (count, size, wide)], own, half, q,
    )
    seen = []
    for step in steps[:-2]:
        body = state_step_kernel if seen else without(state_step_kernel, 3)
        got = exchange(total, step)
        total, after = call(
            functools.partial(body, step, **sizes), [(size + TAIL, both), (size, both)], total, got, *seen
        )
        seen = [after]
    got = exchange(total, steps[-2])
    sent, after = call(
        functools.partial(state_last_kernel, steps[-2], **sizes),
        [(2 * TAIL, both), (size, both)], total, got, *seen, init, maps,
    )
    maps, offsets = call(
        functools.partial(reach_state_kernel, **sizes, nu=nu),
        [halves(count, width, 2 * wide), (count, TAIL, wide)], maps, after,
    )
    got = exchange(sent, steps[-1])
    states, controls, decrease = call(
        functools.partial(rollout_kernel, knots, steps[-1]),
        [(count, trajs, width), (count, trajs, nu), (1, trajs)],
        sent, got, init, maps, offsets,
    )
    return new_gains, feedforward, states, controls, decrease.reshape(trajs)


def solution(mesh):
    in_specs = (
        P("tm", "grp", None, None),
        P("tm", "grp", None, None),
        P("tm", "grp", None, None),
        P("tm", "grp", None),
        P("tm", "grp", None),
        P("tm", "grp", None),
        P(),
        P(),
        P("grp", None),
    )
    out_specs = (
        P("tm", "grp", None, None),
        P("tm", "grp", None),
        P("tm", "grp", None),
        P("tm", "grp", None),
        P("grp"),
    )
    return jax.shard_map(shards, mesh=mesh, in_specs=in_specs, out_specs=out_specs, check_vma=False)
```

```python
import functools
import math

import jax
import jax.numpy as jnp
from jax import lax
from jax.experimental import pallas as pl
from jax.experimental.pallas import tpu as pltpu
from jax.sharding import PartitionSpec as P

F32 = jnp.float32
LANES = 128
TAIL = 8


def lane_block(shape, size):
    return lax.broadcasted_iota(jnp.int32, shape, 1) // size


def spread(pair, trajs):
    block = lane_block(pair.shape, pair.shape[1] // trajs)
    return jnp.concatenate([jnp.where(block == j, pair, 0.0) for j in range(trajs)], axis=0)


def split(x):
    high = x.astype(jnp.bfloat16)
    low = (x - high.astype(F32)).astype(jnp.bfloat16)
    return high, low


def left_of(x):
    return jnp.concatenate(split(x), axis=1)


def right_of(x, flip=False):
    depth, wide = (1, 0) if flip else (0, 1)
    both = jnp.concatenate(split(x), axis=wide)
    return jnp.concatenate([both, both], axis=depth)


def product_of(left, right, flip=False):
    dims = (((1,), (1 if flip else 0,)), ((), ()))
    w = lax.dot_general(left, right, dims, preferred_element_type=F32)
    full = w.shape[1] // 2
    return w[:, :full] + w[:, full:]


def prod(left, right, flip=False):
    wide = 0 if flip else 1
    columns = right.shape[wide]
    if columns % LANES:
        shape = list(right.shape)
        shape[wide] = -columns % LANES
        right = jnp.concatenate([right, jnp.zeros(shape, F32)], axis=wide)
    if left.shape[1] % LANES:
        rows, full = left.shape[0], right.shape[wide]
        dims = (((1,), (1 if flip else 0,)), ((), ()))
        w = lax.dot_general(
            jnp.concatenate(split(left), axis=0), jnp.concatenate(split(right), axis=wide), dims,
            preferred_element_type=F32,
        )
        w = w[:rows] + w[rows:]
        w = w[:, :full] + w[:, full:]
    else:
        w = product_of(left_of(left), right_of(right, flip), flip)
    return w[:, :columns]


def tail_of(row):
    shape = (TAIL, row.shape[1])
    return jnp.where(lax.broadcasted_iota(jnp.int32, shape, 0) == 0, jnp.broadcast_to(row, shape), 0.0)


def join(matrix, tail):
    return jnp.concatenate([matrix, tail], axis=0)


def apply_values(maps, later, trajs, width):
    ws = [prod(late, spread(x[:width], trajs), flip=True) for (x, _), late in zip(maps, later)]
    zs = [prod(x, spread(w[:width], trajs)) + y for (x, y), w in zip(maps, ws)]
    return [join(z[:width], z[width:] + w[width:]) for z, w in zip(zs, ws)]


def compose_states(pairs, trajs, width):
    zs = [prod(first, spread(second[:width], trajs)) for first, second in pairs]
    return [join(z[:width], z[width:] + second[width:]) for z, (_, second) in zip(zs, pairs)]


def compose_values(pairs, trajs, width):
    ws = [prod(second[1], spread(first[0][:width], trajs), flip=True) for first, second in pairs]
    xs = compose_states([(first[0], second[0]) for first, second in pairs], trajs, width)
    zs = [prod(first[0], spread(w[:width], trajs)) + first[1] for (first, _), w in zip(pairs, ws)]
    return [(x, join(z[:width], z[width:] + w[width:])) for x, z, w in zip(xs, zs, ws)]


def fold(items, joined):
    while len(items) > 1:
        rest = items[len(items) // 2 * 2 :]
        items = joined([(items[i], items[i + 1]) for i in range(0, len(items) - 1, 2)]) + rest
    return items[0]


def prefixes(items, joined):
    items, step = list(items), 1
    while step < len(items):
        late = [i for i in range(len(items)) if i // step % 2]
        for i, joint in zip(late, joined([(items[i // step * step - 1], items[i]) for i in late])):
            items[i] = joint
        step *= 2
    return items


def identity_pair(width, trajs):
    rows = lax.broadcasted_iota(jnp.int32, (width, width * trajs), 0)
    lanes = lax.broadcasted_iota(jnp.int32, (width, width * trajs), 1)
    return jnp.where(rows == lanes % width, 1.0, 0.0)


def side_by_side(rows, trajs):
    return jnp.concatenate([rows[:, j] for j in range(trajs)], axis=1)


def term_of(cost_factor, trajs):
    width = cost_factor.shape[0]
    return prod(cost_factor, jnp.concatenate([cost_factor] * trajs, axis=0), flip=True) + identity_pair(width, trajs)


def paired(parts):
    return jnp.concatenate([parts[j] for j in range(parts.shape[0])], axis=1)


def block_kernel(knots, *refs):
    sources, (total_ref, own_ref, term_ref, at_ref, btp_ref), held, sems = refs[:8], refs[8:13], refs[13:21], refs[21]
    copies = [pltpu.make_async_copy(a, b, sems.at[i]) for i, (a, b) in enumerate(zip(sources, held))]
    order = (7, 2, 1, 6, 3, 4, 5, 0)
    for i in order:
        copies[i].start()
    a_ref, bt_ref, g_ref, d_ref, sg_ref, cg_ref, cf_ref, rf_ref = held
    count, trajs, nu, width = bt_ref.shape
    both = trajs * width
    scale = 1.0 / math.sqrt(knots)
    rows = lax.broadcasted_iota(jnp.int32, (nu, nu), 0)
    lanes = lax.broadcasted_iota(jnp.int32, (nu, nu), 1)
    for i in (7, 2, 1):
        copies[i].wait()
    root = jnp.concatenate([jnp.where(rows == lanes, 1.0, 0.0), rf_ref[...]], axis=1)
    root = spread(jnp.concatenate([root] * trajs, axis=1), trajs)
    pushed = []
    for t in range(count):
        gt = g_ref[t].reshape(trajs * nu, width).T
        btp = paired(bt_ref[t])
        btp_ref[t] = btp
        pushed.append(prod(gt, jnp.concatenate([spread(btp, trajs), root], axis=1)))
    for i in (6, 3, 4, 5):
        copies[i].wait()
    term = term_of(cf_ref[...], trajs)
    run_q = term / knots
    term_ref[...] = join(term, jnp.zeros((TAIL, both), F32))
    drift = side_by_side(d_ref[...], trajs) * scale
    grad = side_by_side(sg_ref[...], trajs) * scale
    cg = cg_ref[...]
    nothing = jnp.zeros((count, nu), F32)
    control = jnp.concatenate([piece for j in range(trajs) for piece in (cg[:, j], nothing)], axis=1)
    zs = [w[:, both:] for w in pushed]
    ys = [prod(join(z, tail_of(control[t : t + 1])), spread(z, trajs), flip=True) for t, z in enumerate(zs)]
    ys = [y + join(run_q, tail_of(grad[t : t + 1])) for t, y in enumerate(ys)]
    copies[0].wait()
    maps = []
    for t, (w, y) in enumerate(zip(pushed, ys)):
        at = a_ref[t].reshape(both, width).T
        at_ref[t] = at
        x = join(at + w[:, :both], tail_of(drift[t : t + 1]))
        own_ref[t, 0] = x
        own_ref[t, 1] = y
        maps.append((x, y))
    befores = prefixes([x for x, _ in maps], lambda pairs: compose_states(pairs, trajs, width))
    nothing = jnp.zeros_like(maps[0][1])
    parts = apply_values([(x, nothing) for x in befores[:-1]], [y for _, y in maps[1:]], trajs, width)
    total_ref[0] = befores[-1]
    total_ref[1] = functools.reduce(jnp.add, parts, maps[0][1])


def suffix_kernel(own_ref, *refs, trajs, width):
    out_ref, count = refs[-1], own_ref.shape[0]
    maps = [(own_ref[t, 0], own_ref[t, 1]) for t in reversed(range(1, count))]
    done = prefixes(maps, lambda pairs: compose_values([(b, a) for a, b in pairs], trajs, width))
    for i, (x, y) in enumerate(done):
        out_ref[count - 2 - i, 0] = x
        out_ref[count - 2 - i, 1] = y


def prepare_kernel(
    knots, at_ref, btp_ref, d_ref, cg_ref, rf_ref, x_ref,
    left_ref, hess_ref, cross_ref, gain_ref, bd_ref, ad_ref, run_r_ref, control_ref, init_ref,
):
    count, nu, both = btp_ref.shape
    trajs, width = x_ref.shape
    stack = trajs * nu
    group = LANES // stack
    init_ref[...] = tail_of(jnp.concatenate([x_ref[j : j + 1] for j in range(trajs)], axis=1))
    drift = side_by_side(d_ref[...], trajs) * (1.0 / math.sqrt(knots))
    control_ref[...] = side_by_side(cg_ref[...], trajs).T
    rf = rf_ref[...]
    rows = lax.broadcasted_iota(jnp.int32, (nu, nu), 0)
    lanes = lax.broadcasted_iota(jnp.int32, (nu, nu), 1)
    run_r = prod(rf, rf, flip=True) + jnp.where(rows == lanes, 1.0, 0.0)
    run_r_ref[...] = jnp.concatenate([run_r] * (LANES // nu), axis=1)
    spare = jnp.zeros((left_ref.shape[1] - nu - TAIL - width, both), F32)
    bds = []
    for t in range(count):
        at, btp = at_ref[t], btp_ref[t]
        bd = spread(btp, trajs)
        bds.append(bd)
        tail = tail_of(drift[t : t + 1])
        left_ref[t] = left_of(jnp.concatenate([btp, tail, at, spare], axis=0))
        hess_ref[t] = placed(bd, t % group, group)
        cross_ref[t] = right_of(over(at), flip=True)
        bd_ref[t] = bd
        ad_ref[t] = join(at, tail)
        if len(bds) == group:
            gain_ref[t // group] = right_of(jnp.concatenate(bds, axis=0))
            bds = []


def placed(bd, at, group):
    return right_of(jnp.concatenate([bd if i == at else jnp.zeros_like(bd) for i in range(group)], axis=0), flip=True)


def over(matrix):
    return jnp.concatenate([matrix, jnp.zeros((-matrix.shape[0] % LANES, matrix.shape[1]), F32)], axis=0)


def reach_kernel(
    suffix_ref, seen_ref, left_ref, hess_ref, cross_ref, bd_ref, run_r_ref, control_ref,
    value_out, hess_out, cross_out, bd_out, hess_base, cross_base, *, trajs, width,
):
    count, nu = left_ref.shape[0], run_r_ref.shape[0]
    group = count // hess_base.shape[0]
    seen = (seen_ref[0], seen_ref[1])
    maps = compose_values([((suffix_ref[t, 0], suffix_ref[t, 1]), seen) for t in range(count - 1)], trajs, width)
    maps.append(seen)
    both = trajs * width
    rows = value_out.shape[1]
    firsts = [product_of(left_ref[t], right_of(spread(x[:width], trajs))) for t, (x, _) in enumerate(maps)]
    us = [product_of(left_ref[t, :rows], right_of(spread(y[:width], trajs))) for t, (_, y) in enumerate(maps)]
    hesses = [product_of(left_of(u[:nu]), hess_ref[t], flip=True) for t, u in enumerate(us)]
    crosses = [product_of(left_of(spread(u[:nu], trajs)), cross_ref[t], flip=True) for t, u in enumerate(us)]
    lin_lane = lax.broadcasted_iota(jnp.int32, crosses[0].shape, 1) == width
    spare = jnp.zeros((rows - nu - TAIL, both), F32)
    for t, (w, (x, y)) in enumerate(zip(firsts, maps)):
        bd = spread(w[:nu], trajs)
        value_out[t] = left_of(jnp.concatenate([w[:nu], w[nu : nu + TAIL] + x[width:], spare], axis=0))
        hess_out[t] = placed(bd, t % group, group)
        cross_out[t] = right_of(over(w[nu + TAIL : nu + TAIL + width]), flip=True)
        bd_out[t] = bd
        vector = us[t][nu : nu + 1] + y[width : width + 1]
        lin = jnp.sum(bd_ref[t] * vector, axis=1, keepdims=True) + control_ref[:, t : t + 1]
        cross_base[t] = jnp.where(lin_lane, lin, crosses[t])
    for g in range(count // group):
        hess_base[g] = functools.reduce(jnp.add, hesses[g * group : (g + 1) * group], run_r_ref[...])


def upper(step):
    return lax.rem(lax.axis_index("tm") // step, 2) == 1


def value_step_kernel(step, own_ref, got_ref, seen_ref, *refs, trajs, width):
    total_ref, next_ref = refs[-2:]
    up = upper(step)
    own, got = (own_ref[0], own_ref[1]), (got_ref[0], got_ref[1])
    first = [jnp.where(up, g, o) for o, g in zip(own, got)]
    second = [jnp.where(up, o, g) for o, g in zip(own, got)]
    if seen_ref is None:
        seen = (join(identity_pair(width, trajs), jnp.zeros((TAIL, trajs * width), F32)), jnp.zeros_like(own[0]))
        (x, y), = compose_values([(first, second)], trajs, width)
        after = got
    else:
        seen = (seen_ref[0], seen_ref[1])
        (x, y), after = compose_values([(first, second), (seen, got)], trajs, width)
    total_ref[0] = x
    total_ref[1] = y
    next_ref[0] = jnp.where(up, seen[0], after[0])
    next_ref[1] = jnp.where(up, seen[1], after[1])


def value_last_kernel(step, own_ref, got_ref, seen_ref, term_ref, *refs, trajs, width):
    up = upper(step)
    own, got = (own_ref[0], own_ref[1]), (got_ref[0], got_ref[1])
    first = [jnp.where(up, g, o) for o, g in zip(own, got)]
    second = [jnp.where(up, o, g) for o, g in zip(own, got)]
    value_ref, next_ref = refs[-2:]
    seen, term = (seen_ref[0], seen_ref[1]), term_ref[...]
    total, (sx, sy) = compose_values([(first, second), (seen, got)], trajs, width)
    value_ref[...], = apply_values([total], [term], trajs, width)
    next_ref[0] = jnp.where(up, seen[0], sx)
    next_ref[1] = jnp.where(up, seen[1], sy)


def factors(packs, size):
    block, step = 8, 4
    rows = lax.broadcasted_iota(jnp.int32, (block, LANES), 0)
    lanes = lax.broadcasted_iota(jnp.int32, (block, LANES), 1)
    inner = lanes % size
    first = lanes - inner
    packs = [[pack[i : i + block] for i in range(0, size, block)] for pack in packs]
    ws = [[jnp.zeros((block, LANES), F32) for _ in pack] for pack in packs]
    qs = [list(w) for w in ws]
    for k in range(0, size, step):
        at, r = k // block, k % block
        inside = (inner >= k) & (inner < k + step)
        known = inner[:1] < k + step
        for number, pack in enumerate(packs):
            columns = {
                i: [jnp.take_along_axis(pack[i], first + (k + j), axis=1) for j in range(step)]
                for i in range(at, len(pack))
            }
            p = [[columns[at][j][r + i : r + i + 1] for j in range(step)] for i in range(step)]
            z = [
                jnp.where(inside[:1], jnp.where(inner[:1] == k + i, 1.0, 0.0), pack[at][r + i : r + i + 1])
                for i in range(step)
            ]
            for i in range(step):
                ws[number][at] = jnp.where(rows == r + i, jnp.where(known, z[i], 0.0), ws[number][at])
            inverse = []
            for i in range(step):
                inverse.append(1.0 / p[i][i])
                for j in range(i + 1, step):
                    ratio = p[j][i] * inverse[i]
                    for c in range(i + 1, step):
                        p[j][c] = p[j][c] - ratio * p[i][c]
                    z[j] = z[j] - ratio * z[i]
            q = [None] * step
            for i in reversed(range(step)):
                v = z[i]
                for j in range(i + 1, step):
                    v = v - p[i][j] * q[j]
                q[i] = v * inverse[i]
            for i in range(step):
                qs[number][at] = jnp.where(rows == r + i, jnp.where(known, q[i], 0.0), qs[number][at])
            for i in range(at if r + step < block else at + 1, len(pack)):
                y = jnp.where(inside, 0.0, pack[i])
                for j in range(step):
                    y = y - columns[i][j] * q[j]
                pack[i] = y
    return [(jnp.concatenate(w, axis=0), jnp.concatenate(q, axis=0)) for w, q in zip(ws, qs)]


def solve_kernel(
    step, term_ref, end_ref, value_ref, hess_ref, cross_ref, bd_ref, hess_base, cross_base, gain_ref, ad_ref,
    total_ref, own_ref, half_ref, q_ref,
):
    count, stack, both = bd_ref.shape
    size = ad_ref.shape[1]
    groups, nu, _ = hess_base.shape
    width = size - TAIL
    trajs, group = both // width, count // groups
    rows = value_ref.shape[1]
    lin_lane = lax.broadcasted_iota(jnp.int32, (stack, LANES), 1) == width

    end = jnp.where(upper(step), term_ref[...], end_ref[...])
    w = product_of(value_ref[...].reshape(count * rows, 2 * both), right_of(spread(end[:width], trajs)))
    us = [w[t * rows : t * rows + nu] for t in range(count)]
    hesses = [product_of(left_of(u), hess_ref[t], flip=True) for t, u in enumerate(us)]
    hesses = [functools.reduce(jnp.add, hesses[g * group : (g + 1) * group], hess_base[g]) for g in range(groups)]
    pairs = factors(hesses, nu)
    crosses = [product_of(left_of(spread(u, trajs)), cross_ref[t], flip=True) for t, u in enumerate(us)]
    systems = []
    for t, cross in enumerate(crosses):
        vector = w[t * rows + nu : t * rows + nu + 1] + end[width : width + 1]
        lin = jnp.sum(bd_ref[t] * vector, axis=1, keepdims=True)
        systems.append(jnp.where(lin_lane, lin, cross) + cross_base[t])

    flats = [jnp.concatenate(systems[t : t + group], axis=0).T[:size] for t in range(0, count, group)]
    lefts = [left_of(flat) for flat in flats]
    lanes = lax.broadcasted_iota(jnp.int32, (1, LANES), 1)
    spreads = [(spread(w, LANES // nu), spread(q, LANES // nu)) for w, q in pairs]
    halves = [product_of(left, right_of(w, flip=True), flip=True) for left, (w, _) in zip(lefts, spreads)]
    pushes = [product_of(left_of(q), gain_ref[g]) for g, (_, q) in enumerate(spreads)]
    maps = []
    for g, half in enumerate(halves):
        left = left_of(half)
        for i in range(group):
            mine = pushes[g][i * stack : (i + 1) * stack]
            pieces = [mine if k == i else jnp.zeros_like(mine) for k in range(group)]
            maps.append(ad_ref[g * group + i] - product_of(left, right_of(jnp.concatenate(pieces, axis=0))))
    total_ref[:size] = fold(maps, lambda pairs: compose_states(pairs, trajs, width))
    for t, m in enumerate(maps):
        own_ref[t] = m

    decrease = jnp.zeros((1, LANES), F32)
    for g, (half, flat) in enumerate(zip(halves, flats)):
        half_ref[g] = half
        q_ref[g] = pairs[g][1]
        feed = -prod(half[width:], spreads[g][1])[:1]
        feed_columns = jnp.broadcast_to(feed, (TAIL, LANES)).T
        weights = jnp.zeros((nu, LANES), F32)
        for at in range(LANES // nu):
            column = feed_columns[at * nu : (at + 1) * nu, :1]
            weights = jnp.where((lanes >= at * nu) & (lanes < (at + 1) * nu), column, weights)
        pushed = jnp.sum(weights * hesses[g], axis=0, keepdims=True)
        decrease = decrease + feed * flat[width : width + 1] + 0.5 * (feed * pushed)
    total_ref[size:] = tail_of(decrease)


def expand_kernel(
    own_ref, half_ref, q_ref, gain_ref, feed_ref, map_ref, *, trajs, width
):
    count, size, both = own_ref.shape
    groups, nu, _ = q_ref.shape
    group, stack = count // groups, trajs * nu
    gains = []
    kts = [-prod(half_ref[g], spread(q_ref[g], LANES // nu)) for g in range(groups)]
    for g, kt in enumerate(kts):
        spare = jnp.zeros((LANES - size, LANES), F32)
        natural = join(kt, spare).T
        for i in range(group):
            t = g * group + i
            gain_ref[t] = natural[i * stack : (i + 1) * stack, :width].reshape(trajs, nu, width)
            for j in range(trajs):
                at = i * stack + j * nu
                feed_ref[t : t + 1, j] = kt[width : width + 1, at : at + nu]
            gains.append(kt[:, i * stack : (i + 1) * stack])
    maps = [own_ref[t] for t in range(count - 1)]
    done = prefixes(maps, lambda pairs: compose_states(pairs, trajs, width))
    start = join(identity_pair(width, trajs), jnp.zeros((TAIL, both), F32))
    controls = [prod(m, spread(kt[:width], trajs)) for m, kt in zip(done, gains[1:])]
    controls = [join(u[:width], u[width:] + kt[width:]) for u, kt in zip(controls, gains[1:])]
    for t, (m, control) in enumerate(zip([start] + done, gains[:1] + controls)):
        map_ref[t] = jnp.concatenate([m, control, jnp.zeros((size, -stack % LANES), F32)], axis=1)


def reach_state_kernel(map_ref, seen_ref, out_ref, offset_ref, *, trajs, width, nu):
    seen = seen_ref[...]
    rows = jnp.concatenate([seen[:, j * width : (j + 1) * width] for j in range(trajs)], axis=0)
    size, both = seen.shape
    tails = map_ref[:, width:]
    products = [prod(rows, map_ref[t, :width]) for t in range(map_ref.shape[0])]
    for t, w in enumerate(products):
        lane = lax.broadcasted_iota(jnp.int32, (size, w.shape[1]), 1)
        owner = jnp.where(lane < both, lane // width, (lane - both) // nu)
        full = w[:size]
        for j in range(1, trajs):
            full = jnp.where(owner >= j, w[j * size : (j + 1) * size], full)
        out_ref[t] = jnp.concatenate(split(full[:width]), axis=1)
        offset_ref[t] = full[width:] + tails[t]


def state_step_kernel(step, own_ref, got_ref, seen_ref, total_ref, next_ref, *, trajs, width):
    up = upper(step)
    size = width + TAIL
    own, got = own_ref[:size], got_ref[:size]
    total_ref[size:] = own_ref[size:] + got_ref[size:]
    pair = (jnp.where(up, got, own), jnp.where(up, own, got))
    if seen_ref is None:
        seen = join(identity_pair(width, trajs), jnp.zeros((TAIL, trajs * width), F32))
        total_ref[:size], = compose_states([pair], trajs, width)
        after = got
    else:
        seen = seen_ref[...]
        total_ref[:size], after = compose_states([pair, (got, seen)], trajs, width)
    next_ref[...] = jnp.where(up, after, seen)


def state_last_kernel(step, own_ref, got_ref, seen_ref, init_ref, *refs, trajs, width):
    sent_ref, next_ref = refs[-2:]
    up = upper(step)
    size = width + TAIL
    own, got = own_ref[:size], got_ref[:size]
    seen = seen_ref[...]
    pair = (jnp.where(up, got, own), jnp.where(up, own, got))
    total, after = compose_states([pair, (got, seen)], trajs, width)
    sent_ref[:TAIL] = prod(init_ref[...], spread(total[:width], trajs)) + total[width:]
    sent_ref[TAIL:] = own_ref[size:] + got_ref[size:]
    next_ref[...] = jnp.where(up, after, seen)


def rows_times(row, right, trajs):
    width = right.shape[0]
    rows = jnp.concatenate([row[:1, j * width : (j + 1) * width] for j in range(trajs)], axis=0)
    left = jnp.concatenate(split(rows), axis=0)
    w = lax.dot_general(left, right, (((1,), (0,)), ((), ())), preferred_element_type=F32)
    w = w[:trajs] + w[trajs:]
    full = w.shape[1] // 2
    return w[:, :full] + w[:, full:]


def rollout_kernel(knots, step, own_ref, got_ref, init_ref, map_ref, offset_ref,
                   state_ref, control_ref, decrease_ref):
    count, trajs, width = state_ref.shape
    nu = control_ref.shape[2]
    both = trajs * width
    start = jnp.where(upper(step), got_ref[:1], init_ref[:1])
    for t in range(count):
        w = rows_times(start, map_ref[t], trajs) + offset_ref[t, :1]
        for j in range(trajs):
            state_ref[t : t + 1, j] = w[j : j + 1, j * width : (j + 1) * width]
            control_ref[t : t + 1, j] = w[j : j + 1, both + j * nu : both + (j + 1) * nu]
    sums = (own_ref[TAIL : TAIL + 1] + got_ref[TAIL : TAIL + 1]) / knots
    lane = lax.broadcasted_iota(jnp.int32, sums.shape, 1) // nu % trajs
    for j in range(trajs):
        decrease_ref[:, j : j + 1] = jnp.sum(jnp.where(lane == j, sums, 0.0), axis=1, keepdims=True)


def call(body, outs, *args, **named):
    return pl.pallas_call(
        body,
        out_shape=[
            jax.ShapeDtypeStruct(shape, F32) if isinstance(shape, tuple) else shape for shape in outs
        ],
        compiler_params=pltpu.CompilerParams(vmem_limit_bytes=32 * 1024 * 1024),
        **named,
    )(*args)


def halves(*shape):
    return jax.ShapeDtypeStruct(shape, jnp.bfloat16)


def without(body, at):
    @functools.wraps(body)
    def inner(*refs, **named):
        return body(*refs[:at], None, *refs[at:], **named)

    return inner


def unread(wanted, *values):
    return values if wanted else ()


def shards(dyn_a, dyn_b, gains, defects, state_grad, control_grad, cost_factor, control_factor, init_state):
    count, trajs, width, nu = dyn_b.shape
    devices = lax.axis_size("tm")
    knots = count * devices
    both, size = trajs * width, width + TAIL
    sizes = dict(trajs=trajs, width=width)
    steps = [1 << i for i in range(devices.bit_length() - 1)]

    def exchange(value, step, turn=1):
        apart = step ^ turn if step > 1 else step
        return lax.ppermute(value, "tm", [(i, i ^ apart) for i in range(devices)])

    stack = trajs * nu
    groups, up16 = count * stack // LANES, lambda n: -(-n // 16) * 16
    bt = jnp.swapaxes(dyn_b, 2, 3)
    inputs = (dyn_a, bt, gains, defects, state_grad, control_grad, cost_factor, control_factor)
    total, own, term, at, btp = call(
        functools.partial(block_kernel, knots),
        [(2, size, both), (count, 2, size, both), (size, both), (count, width, both), (count, nu, both)],
        *[pltpu.with_memory_space_constraint(x, pltpu.HBM) for x in inputs],
        in_specs=[pl.BlockSpec(memory_space=pltpu.HBM)] * len(inputs),
        scratch_shapes=[pltpu.VMEM(x.shape, F32) for x in inputs] + [pltpu.SemaphoreType.DMA((len(inputs),))],
    )
    suffix, = call(functools.partial(suffix_kernel, **sizes), [(count - 1, 2, size, both)], own)
    turned = (count, 2 * LANES, 2 * both)
    left, hess, cross, gain, bd, ad, run_r, control, init = call(
        functools.partial(prepare_kernel, knots),
        [halves(count, up16(nu + TAIL + width), 2 * both), halves(*turned), halves(*turned),
         halves(groups, *turned[1:]), (count, stack, both), (count, size, both), (nu, LANES), (stack, count),
         (TAIL, both)],
        at, btp, defects, control_grad, control_factor, init_state,
    )
    got = exchange(total, steps[0])
    total, after = call(
        functools.partial(without(value_step_kernel, 3), steps[0], **sizes), [(2, size, both)] * 2, total, got
    )
    for i, step in enumerate(steps[1:-2]):
        got = exchange(total, step)
        total, after = call(
            functools.partial(value_step_kernel, step, **sizes), [(2, size, both)] * 2,
            total, got, after, *unread(i == 0, init),
        )
    got = exchange(total, steps[-2], turn=0)
    value, after = call(
        functools.partial(value_last_kernel, steps[-2], **sizes),
        [(size, both), (2, size, both)], total, got, after, term, suffix,
    )
    reach = call(
        functools.partial(reach_kernel, **sizes),
        [halves(count, up16(nu + TAIL), 2 * both), halves(*turned), halves(*turned), (count, stack, both),
         (groups, nu, LANES), (count, stack, LANES)],
        suffix, after, left, hess, cross, bd, run_r, control,
    )
    value = exchange(value, steps[-1])
    total, own, half, q = call(
        functools.partial(solve_kernel, steps[-1]),
        [(size + TAIL, both), (count, size, both), (groups, size, LANES), (groups, nu, LANES)],
        term, value, *reach, gain, ad,
    )
    wide = both + -(-stack // LANES) * LANES
    new_gains, feedforward, maps = call(
        functools.partial(expand_kernel, **sizes),
        [(count, trajs, nu, width), (count, trajs, nu), (count, size, wide)], own, half, q,
    )
    seen = []
    for step in steps[:-2]:
        body = state_step_kernel if seen else without(state_step_kernel, 3)
        got = exchange(total, step)
        total, after = call(
            functools.partial(body, step, **sizes), [(size + TAIL, both), (size, both)], total, got, *seen
        )
        seen = [after]
    got = exchange(total, steps[-2])
    sent, after = call(
        functools.partial(state_last_kernel, steps[-2], **sizes),
        [(2 * TAIL, both), (size, both)], total, got, *seen, init, maps,
    )
    maps, offsets = call(
        functools.partial(reach_state_kernel, **sizes, nu=nu),
        [halves(count, width, 2 * wide), (count, TAIL, wide)], maps, after,
    )
    got = exchange(sent, steps[-1])
    states, controls, decrease = call(
        functools.partial(rollout_kernel, knots, steps[-1]),
        [(count, trajs, width), (count, trajs, nu), (1, trajs)],
        sent, got, init, maps, offsets,
    )
    return new_gains, feedforward, states, controls, decrease.reshape(trajs)


def solution(mesh):
    in_specs = (
        P("tm", "grp", None, None),
        P("tm", "grp", None, None),
        P("tm", "grp", None, None),
        P("tm", "grp", None),
        P("tm", "grp", None),
        P("tm", "grp", None),
        P(),
        P(),
        P("grp", None),
    )
    out_specs = (
        P("tm", "grp", None, None),
        P("tm", "grp", None),
        P("tm", "grp", None),
        P("tm", "grp", None),
        P("grp"),
    )
    return jax.shard_map(shards, mesh=mesh, in_specs=in_specs, out_specs=out_specs, check_vma=False)
```

```python
import functools
import math

import jax
import jax.numpy as jnp
from jax import lax
from jax.experimental import pallas as pl
from jax.experimental.pallas import tpu as pltpu
from jax.sharding import PartitionSpec as P

F32 = jnp.float32
LANES = 128
TAIL = 8


def lane_block(shape, size):
    return lax.broadcasted_iota(jnp.int32, shape, 1) // size


def spread(pair, trajs):
    block = lane_block(pair.shape, pair.shape[1] // trajs)
    return jnp.concatenate([jnp.where(block == j, pair, 0.0) for j in range(trajs)], axis=0)


def split(x):
    high = x.astype(jnp.bfloat16)
    low = (x - high.astype(F32)).astype(jnp.bfloat16)
    return high, low


def left_of(x):
    return jnp.concatenate(split(x), axis=1)


def right_of(x, flip=False):
    depth, wide = (1, 0) if flip else (0, 1)
    both = jnp.concatenate(split(x), axis=wide)
    return jnp.concatenate([both, both], axis=depth)


def product_of(left, right, flip=False):
    dims = (((1,), (1 if flip else 0,)), ((), ()))
    w = lax.dot_general(left, right, dims, preferred_element_type=F32)
    full = w.shape[1] // 2
    return w[:, :full] + w[:, full:]


def prod(left, right, flip=False):
    wide = 0 if flip else 1
    columns = right.shape[wide]
    if columns % LANES:
        shape = list(right.shape)
        shape[wide] = -columns % LANES
        right = jnp.concatenate([right, jnp.zeros(shape, F32)], axis=wide)
    if left.shape[1] % LANES:
        rows, full = left.shape[0], right.shape[wide]
        dims = (((1,), (1 if flip else 0,)), ((), ()))
        w = lax.dot_general(
            jnp.concatenate(split(left), axis=0), jnp.concatenate(split(right), axis=wide), dims,
            preferred_element_type=F32,
        )
        w = w[:rows] + w[rows:]
        w = w[:, :full] + w[:, full:]
    else:
        w = product_of(left_of(left), right_of(right, flip), flip)
    return w[:, :columns]


def tail_of(row):
    shape = (TAIL, row.shape[1])
    return jnp.where(lax.broadcasted_iota(jnp.int32, shape, 0) == 0, jnp.broadcast_to(row, shape), 0.0)


def alone(tail):
    return jnp.where(lax.broadcasted_iota(jnp.int32, tail.shape, 0) == 0, tail, 0.0)


def with_second(tail, row):
    return jnp.where(lax.broadcasted_iota(jnp.int32, tail.shape, 0) == 1, jnp.broadcast_to(row, tail.shape), tail)


def one_piece(x, y, width):
    return jnp.concatenate([x[:width], y[:width], with_second(x[width:], y[width : width + 1])], axis=0)


def two_pieces(sent, width):
    tail = sent[2 * width :]
    return join(sent[:width], alone(tail)), join(sent[width : 2 * width], tail_of(tail[1:2]))


def join(matrix, tail):
    return jnp.concatenate([matrix, tail], axis=0)


def apply_values(maps, later, trajs, width):
    ws = [prod(late, spread(x[:width], trajs), flip=True) for (x, _), late in zip(maps, later)]
    zs = [prod(x, spread(w[:width], trajs)) + y for (x, y), w in zip(maps, ws)]
    return [join(z[:width], z[width:] + w[width:]) for z, w in zip(zs, ws)]


def compose_states(pairs, trajs, width):
    zs = [prod(first, spread(second[:width], trajs)) for first, second in pairs]
    return [join(z[:width], z[width:] + second[width:]) for z, (_, second) in zip(zs, pairs)]


def compose_values(pairs, trajs, width):
    ws = [prod(second[1], spread(first[0][:width], trajs), flip=True) for first, second in pairs]
    xs = compose_states([(first[0], second[0]) for first, second in pairs], trajs, width)
    zs = [prod(first[0], spread(w[:width], trajs)) + first[1] for (first, _), w in zip(pairs, ws)]
    return [(x, join(z[:width], z[width:] + w[width:])) for x, z, w in zip(xs, zs, ws)]


def fold(items, joined):
    while len(items) > 1:
        rest = items[len(items) // 2 * 2 :]
        items = joined([(items[i], items[i + 1]) for i in range(0, len(items) - 1, 2)]) + rest
    return items[0]


def prefixes(items, joined):
    items, step = list(items), 1
    while step < len(items):
        late = [i for i in range(len(items)) if i // step % 2]
        for i, joint in zip(late, joined([(items[i // step * step - 1], items[i]) for i in late])):
            items[i] = joint
        step *= 2
    return items


def identity_pair(width, trajs):
    rows = lax.broadcasted_iota(jnp.int32, (width, width * trajs), 0)
    lanes = lax.broadcasted_iota(jnp.int32, (width, width * trajs), 1)
    return jnp.where(rows == lanes % width, 1.0, 0.0)


def side_by_side(rows, trajs):
    return jnp.concatenate([rows[:, j] for j in range(trajs)], axis=1)


def term_of(cost_factor, trajs):
    width = cost_factor.shape[0]
    return prod(cost_factor, jnp.concatenate([cost_factor] * trajs, axis=0), flip=True) + identity_pair(width, trajs)


def paired(parts):
    return jnp.concatenate([parts[j] for j in range(parts.shape[0])], axis=1)


def block_kernel(knots, *refs):
    sources, (total_ref, own_ref, term_ref, at_ref, btp_ref), held, sems = refs[:8], refs[8:13], refs[13:21], refs[21]
    copies = [pltpu.make_async_copy(a, b, sems.at[i]) for i, (a, b) in enumerate(zip(sources, held))]
    order = (7, 2, 1, 6, 3, 4, 5, 0)
    for i in order:
        copies[i].start()
    a_ref, bt_ref, g_ref, d_ref, sg_ref, cg_ref, cf_ref, rf_ref = held
    count, trajs, nu, width = bt_ref.shape
    both = trajs * width
    scale = 1.0 / math.sqrt(knots)
    rows = lax.broadcasted_iota(jnp.int32, (nu, nu), 0)
    lanes = lax.broadcasted_iota(jnp.int32, (nu, nu), 1)
    for c in copies:
        c.wait()
    root = jnp.concatenate([jnp.where(rows == lanes, 1.0, 0.0), rf_ref[...]], axis=1)
    root = spread(jnp.concatenate([root] * trajs, axis=1), trajs)
    pushed = []
    for t in range(count):
        gt = g_ref[t].reshape(trajs * nu, width).T
        btp = paired(bt_ref[t])
        btp_ref[t] = btp
        pushed.append(prod(gt, jnp.concatenate([spread(btp, trajs), root], axis=1)))
    term = term_of(cf_ref[...], trajs)
    run_q = term / knots
    term_ref[...] = join(term, jnp.zeros((TAIL, both), F32))
    drift = side_by_side(d_ref[...], trajs) * scale
    grad = side_by_side(sg_ref[...], trajs) * scale
    cg = cg_ref[...]
    nothing = jnp.zeros((count, nu), F32)
    control = jnp.concatenate([piece for j in range(trajs) for piece in (cg[:, j], nothing)], axis=1)
    zs = [w[:, both:] for w in pushed]
    ys = [prod(join(z, tail_of(control[t : t + 1])), spread(z, trajs), flip=True) for t, z in enumerate(zs)]
    ys = [y + join(run_q, tail_of(grad[t : t + 1])) for t, y in enumerate(ys)]
    maps = []
    for t, (w, y) in enumerate(zip(pushed, ys)):
        at = a_ref[t].reshape(both, width).T
        at_ref[t] = at
        x = join(at + w[:, :both], tail_of(drift[t : t + 1]))
        own_ref[t, 0] = x
        own_ref[t, 1] = y
        maps.append((x, y))
    befores = prefixes([x for x, _ in maps], lambda pairs: compose_states(pairs, trajs, width))
    nothing = jnp.zeros_like(maps[0][1])
    parts = apply_values([(x, nothing) for x in befores[:-1]], [y for _, y in maps[1:]], trajs, width)
    total_ref[...] = one_piece(befores[-1], functools.reduce(jnp.add, parts, maps[0][1]), width)


def suffix_kernel(own_ref, *refs, trajs, width):
    out_ref, count = refs[-1], own_ref.shape[0]
    maps = [(own_ref[t, 0], own_ref[t, 1]) for t in reversed(range(1, count))]
    done = prefixes(maps, lambda pairs: compose_values([(b, a) for a, b in pairs], trajs, width))
    for i, (x, y) in enumerate(done):
        out_ref[count - 2 - i, 0] = x
        out_ref[count - 2 - i, 1] = y


def prepare_kernel(
    knots, at_ref, btp_ref, d_ref, cg_ref, rf_ref, x_ref,
    left_ref, hess_ref, cross_ref, gain_ref, bd_ref, ad_ref, run_r_ref, control_ref, init_ref,
):
    count, nu, both = btp_ref.shape
    trajs, width = x_ref.shape
    stack = trajs * nu
    group = LANES // stack
    init_ref[...] = tail_of(jnp.concatenate([x_ref[j : j + 1] for j in range(trajs)], axis=1))
    drift = side_by_side(d_ref[...], trajs) * (1.0 / math.sqrt(knots))
    control_ref[...] = side_by_side(cg_ref[...], trajs).T
    rf = rf_ref[...]
    rows = lax.broadcasted_iota(jnp.int32, (nu, nu), 0)
    lanes = lax.broadcasted_iota(jnp.int32, (nu, nu), 1)
    run_r = prod(rf, rf, flip=True) + jnp.where(rows == lanes, 1.0, 0.0)
    run_r_ref[...] = jnp.concatenate([run_r] * (LANES // nu), axis=1)
    spare = jnp.zeros((left_ref.shape[1] - nu - TAIL - width, both), F32)
    bds = []
    for t in range(count):
        at, btp = at_ref[t], btp_ref[t]
        bd = spread(btp, trajs)
        bds.append(bd)
        tail = tail_of(drift[t : t + 1])
        left_ref[t] = left_of(jnp.concatenate([btp, tail, at, spare], axis=0))
        hess_ref[t] = placed(bd, t % group, group)
        cross_ref[t] = right_of(over(at), flip=True)
        bd_ref[t] = bd
        ad_ref[t] = join(at, tail)
        if len(bds) == group:
            gain_ref[t // group] = right_of(jnp.concatenate(bds, axis=0))
            bds = []


def placed(bd, at, group):
    return right_of(jnp.concatenate([bd if i == at else jnp.zeros_like(bd) for i in range(group)], axis=0), flip=True)


def over(matrix):
    return jnp.concatenate([matrix, jnp.zeros((-matrix.shape[0] % LANES, matrix.shape[1]), F32)], axis=0)


def reach_kernel(
    step, suffix_ref, got_ref, seen_ref, left_ref, hess_ref, cross_ref, bd_ref, run_r_ref, control_ref,
    value_out, hess_out, cross_out, bd_out, hess_base, cross_base, *, trajs, width,
):
    count, nu = left_ref.shape[0], run_r_ref.shape[0]
    group = count // hess_base.shape[0]
    seen, got = (seen_ref[0], seen_ref[1]), two_pieces(got_ref[...], width)
    after, = compose_values([(seen, got)], trajs, width)
    seen = tuple(jnp.where(upper(step), a, b) for a, b in zip(seen, after))
    maps = compose_values([((suffix_ref[t, 0], suffix_ref[t, 1]), seen) for t in range(count - 1)], trajs, width)
    maps.append(seen)
    both = trajs * width
    rows = value_out.shape[1]
    firsts = [product_of(left_ref[t], right_of(spread(x[:width], trajs))) for t, (x, _) in enumerate(maps)]
    us = [product_of(left_ref[t, :rows], right_of(spread(y[:width], trajs))) for t, (_, y) in enumerate(maps)]
    hesses = [product_of(left_of(u[:nu]), hess_ref[t], flip=True) for t, u in enumerate(us)]
    crosses = [product_of(left_of(spread(u[:nu], trajs)), cross_ref[t], flip=True) for t, u in enumerate(us)]
    lin_lane = lax.broadcasted_iota(jnp.int32, crosses[0].shape, 1) == width
    spare = jnp.zeros((rows - nu - TAIL, both), F32)
    for t, (w, (x, y)) in enumerate(zip(firsts, maps)):
        bd = spread(w[:nu], trajs)
        value_out[t] = left_of(jnp.concatenate([w[:nu], w[nu : nu + TAIL] + x[width:], spare], axis=0))
        hess_out[t] = placed(bd, t % group, group)
        cross_out[t] = right_of(over(w[nu + TAIL : nu + TAIL + width]), flip=True)
        bd_out[t] = bd
        vector = us[t][nu : nu + 1] + y[width : width + 1]
        lin = jnp.sum(bd_ref[t] * vector, axis=1, keepdims=True) + control_ref[:, t : t + 1]
        cross_base[t] = jnp.where(lin_lane, lin, crosses[t])
    for g in range(count // group):
        hess_base[g] = functools.reduce(jnp.add, hesses[g * group : (g + 1) * group], run_r_ref[...])


def upper(step):
    return lax.rem(lax.axis_index("tm") // step, 2) == 1


def value_step_kernel(step, own_ref, got_ref, seen_ref, *refs, trajs, width):
    total_ref, next_ref = refs[-2:]
    up = upper(step)
    own, got = own_ref[...], got_ref[...]
    first, second = two_pieces(jnp.where(up, got, own), width), two_pieces(jnp.where(up, own, got), width)
    got = two_pieces(got, width)
    if seen_ref is None:
        seen = (join(identity_pair(width, trajs), jnp.zeros((TAIL, trajs * width), F32)), jnp.zeros_like(got[1]))
        (x, y), = compose_values([(first, second)], trajs, width)
        after = got
    else:
        seen = (seen_ref[0], seen_ref[1])
        (x, y), after = compose_values([(first, second), (seen, got)], trajs, width)
    total_ref[...] = one_piece(x, y, width)
    next_ref[0] = jnp.where(up, seen[0], after[0])
    next_ref[1] = jnp.where(up, seen[1], after[1])


def value_last_kernel(step, own_ref, got_ref, term_ref, *refs, trajs, width):
    up = upper(step)
    own, got = own_ref[...], got_ref[...]
    first, second = two_pieces(jnp.where(up, got, own), width), two_pieces(jnp.where(up, own, got), width)
    total, = compose_values([(first, second)], trajs, width)
    refs[-1][...], = apply_values([total], [term_ref[...]], trajs, width)


def factors(packs, size):
    block, step = 8, 4
    rows = lax.broadcasted_iota(jnp.int32, (block, LANES), 0)
    lanes = lax.broadcasted_iota(jnp.int32, (block, LANES), 1)
    inner = lanes % size
    first = lanes - inner
    packs = [[pack[i : i + block] for i in range(0, size, block)] for pack in packs]
    ws = [[jnp.zeros((block, LANES), F32) for _ in pack] for pack in packs]
    qs = [list(w) for w in ws]
    for k in range(0, size, step):
        at, r = k // block, k % block
        inside = (inner >= k) & (inner < k + step)
        known = inner[:1] < k + step
        for number, pack in enumerate(packs):
            columns = {
                i: [jnp.take_along_axis(pack[i], first + (k + j), axis=1) for j in range(step)]
                for i in range(at, len(pack))
            }
            p = [[columns[at][j][r + i : r + i + 1] for j in range(step)] for i in range(step)]
            z = [
                jnp.where(inside[:1], jnp.where(inner[:1] == k + i, 1.0, 0.0), pack[at][r + i : r + i + 1])
                for i in range(step)
            ]
            for i in range(step):
                ws[number][at] = jnp.where(rows == r + i, jnp.where(known, z[i], 0.0), ws[number][at])
            inverse = []
            for i in range(step):
                inverse.append(1.0 / p[i][i])
                for j in range(i + 1, step):
                    ratio = p[j][i] * inverse[i]
                    for c in range(i + 1, step):
                        p[j][c] = p[j][c] - ratio * p[i][c]
                    z[j] = z[j] - ratio * z[i]
            q = [None] * step
            for i in reversed(range(step)):
                v = z[i]
                for j in range(i + 1, step):
                    v = v - p[i][j] * q[j]
                q[i] = v * inverse[i]
            for i in range(step):
                qs[number][at] = jnp.where(rows == r + i, jnp.where(known, q[i], 0.0), qs[number][at])
            for i in range(at if r + step < block else at + 1, len(pack)):
                y = jnp.where(inside, 0.0, pack[i])
                for j in range(step):
                    y = y - columns[i][j] * q[j]
                pack[i] = y
    return [(jnp.concatenate(w, axis=0), jnp.concatenate(q, axis=0)) for w, q in zip(ws, qs)]


def solve_kernel(
    step, term_ref, end_ref, value_ref, hess_ref, cross_ref, bd_ref, hess_base, cross_base, gain_ref, ad_ref,
    total_ref, own_ref, half_ref, q_ref,
):
    count, stack, both = bd_ref.shape
    size = ad_ref.shape[1]
    groups, nu, _ = hess_base.shape
    width = size - TAIL
    trajs, group = both // width, count // groups
    rows = value_ref.shape[1]
    lin_lane = lax.broadcasted_iota(jnp.int32, (stack, LANES), 1) == width

    end = jnp.where(upper(step), term_ref[...], end_ref[...])
    w = product_of(value_ref[...].reshape(count * rows, 2 * both), right_of(spread(end[:width], trajs)))
    us = [w[t * rows : t * rows + nu] for t in range(count)]
    hesses = [product_of(left_of(u), hess_ref[t], flip=True) for t, u in enumerate(us)]
    hesses = [functools.reduce(jnp.add, hesses[g * group : (g + 1) * group], hess_base[g]) for g in range(groups)]
    pairs = factors(hesses, nu)
    crosses = [product_of(left_of(spread(u, trajs)), cross_ref[t], flip=True) for t, u in enumerate(us)]
    systems = []
    for t, cross in enumerate(crosses):
        vector = w[t * rows + nu : t * rows + nu + 1] + end[width : width + 1]
        lin = jnp.sum(bd_ref[t] * vector, axis=1, keepdims=True)
        systems.append(jnp.where(lin_lane, lin, cross) + cross_base[t])

    flats = [jnp.concatenate(systems[t : t + group], axis=0).T[:size] for t in range(0, count, group)]
    lefts = [left_of(flat) for flat in flats]
    lanes = lax.broadcasted_iota(jnp.int32, (1, LANES), 1)
    spreads = [(spread(w, LANES // nu), spread(q, LANES // nu)) for w, q in pairs]
    halves = [product_of(left, right_of(w, flip=True), flip=True) for left, (w, _) in zip(lefts, spreads)]
    pushes = [product_of(left_of(q), gain_ref[g]) for g, (_, q) in enumerate(spreads)]
    maps = []
    for g, half in enumerate(halves):
        left = left_of(half)
        for i in range(group):
            mine = pushes[g][i * stack : (i + 1) * stack]
            pieces = [mine if k == i else jnp.zeros_like(mine) for k in range(group)]
            maps.append(ad_ref[g * group + i] - product_of(left, right_of(jnp.concatenate(pieces, axis=0))))
    decrease = jnp.zeros((1, LANES), F32)
    for g, (half, flat) in enumerate(zip(halves, flats)):
        half_ref[g] = half
        q_ref[g] = pairs[g][1]
        feed = -prod(half[width:], spreads[g][1])[:1]
        feed_columns = jnp.broadcast_to(feed, (TAIL, LANES)).T
        weights = jnp.zeros((nu, LANES), F32)
        for at in range(LANES // nu):
            column = feed_columns[at * nu : (at + 1) * nu, :1]
            weights = jnp.where((lanes >= at * nu) & (lanes < (at + 1) * nu), column, weights)
        pushed = jnp.sum(weights * hesses[g], axis=0, keepdims=True)
        decrease = decrease + feed * flat[width : width + 1] + 0.5 * (feed * pushed)
    total = fold(maps, lambda pairs: compose_states(pairs, trajs, width))
    total_ref[...] = join(total[:width], with_second(total[width:], decrease))
    for t, m in enumerate(maps):
        own_ref[t] = m


def expand_kernel(
    own_ref, half_ref, q_ref, gain_ref, feed_ref, map_ref, *, trajs, width
):
    count, size, both = own_ref.shape
    groups, nu, _ = q_ref.shape
    group, stack = count // groups, trajs * nu
    gains = []
    kts = [-prod(half_ref[g], spread(q_ref[g], LANES // nu)) for g in range(groups)]
    for g, kt in enumerate(kts):
        spare = jnp.zeros((LANES - size, LANES), F32)
        natural = join(kt, spare).T
        for i in range(group):
            t = g * group + i
            gain_ref[t] = natural[i * stack : (i + 1) * stack, :width].reshape(trajs, nu, width)
            for j in range(trajs):
                at = i * stack + j * nu
                feed_ref[t : t + 1, j] = kt[width : width + 1, at : at + nu]
            gains.append(kt[:, i * stack : (i + 1) * stack])
    maps = [own_ref[t] for t in range(count - 1)]
    done = prefixes(maps, lambda pairs: compose_states(pairs, trajs, width))
    start = join(identity_pair(width, trajs), jnp.zeros((TAIL, both), F32))
    controls = [prod(m, spread(kt[:width], trajs)) for m, kt in zip(done, gains[1:])]
    controls = [join(u[:width], u[width:] + kt[width:]) for u, kt in zip(controls, gains[1:])]
    for t, (m, control) in enumerate(zip([start] + done, gains[:1] + controls)):
        map_ref[t] = jnp.concatenate([m, control, jnp.zeros((size, -stack % LANES), F32)], axis=1)


def reach_state_kernel(step, map_ref, got_ref, seen_ref, out_ref, offset_ref, *, trajs, width, nu):
    seen = seen_ref[...]
    got = join(got_ref[:width], alone(got_ref[width:]))
    after, = compose_states([(got, seen)], trajs, width)
    seen = jnp.where(upper(step), after, seen)
    rows = jnp.concatenate([seen[:, j * width : (j + 1) * width] for j in range(trajs)], axis=0)
    size, both = seen.shape
    tails = map_ref[:, width:]
    products = [prod(rows, map_ref[t, :width]) for t in range(map_ref.shape[0])]
    for t, w in enumerate(products):
        lane = lax.broadcasted_iota(jnp.int32, (size, w.shape[1]), 1)
        owner = jnp.where(lane < both, lane // width, (lane - both) // nu)
        full = w[:size]
        for j in range(1, trajs):
            full = jnp.where(owner >= j, w[j * size : (j + 1) * size], full)
        out_ref[t] = jnp.concatenate(split(full[:width]), axis=1)
        offset_ref[t] = full[width:] + tails[t]


def state_pair(step, own_ref, got_ref, width):
    up, own, got = upper(step), own_ref[...], got_ref[...]
    ride = own[width + 1 : width + 2] + got[width + 1 : width + 2]
    own, got = join(own[:width], alone(own[width:])), join(got[:width], alone(got[width:]))
    return (jnp.where(up, got, own), jnp.where(up, own, got)), got, ride


def state_step_kernel(step, own_ref, got_ref, seen_ref, total_ref, next_ref, *, trajs, width):
    pair, got, ride = state_pair(step, own_ref, got_ref, width)
    if seen_ref is None:
        seen = join(identity_pair(width, trajs), jnp.zeros((TAIL, trajs * width), F32))
        total, = compose_states([pair], trajs, width)
        after = got
    else:
        seen = seen_ref[...]
        total, after = compose_states([pair, (got, seen)], trajs, width)
    total_ref[...] = join(total[:width], with_second(total[width:], ride))
    next_ref[...] = jnp.where(upper(step), after, seen)


def state_last_kernel(step, own_ref, got_ref, init_ref, *refs, trajs, width):
    pair, _, ride = state_pair(step, own_ref, got_ref, width)
    total, = compose_states([pair], trajs, width)
    state = prod(init_ref[...], spread(total[:width], trajs)) + total[width:]
    refs[-1][...] = with_second(state, ride)


def rows_times(row, right, trajs):
    width = right.shape[0]
    rows = jnp.concatenate([row[:1, j * width : (j + 1) * width] for j in range(trajs)], axis=0)
    left = jnp.concatenate(split(rows), axis=0)
    w = lax.dot_general(left, right, (((1,), (0,)), ((), ())), preferred_element_type=F32)
    w = w[:trajs] + w[trajs:]
    full = w.shape[1] // 2
    return w[:, :full] + w[:, full:]


def rollout_kernel(knots, step, own_ref, got_ref, init_ref, map_ref, offset_ref,
                   state_ref, control_ref, decrease_ref):
    count, trajs, width = state_ref.shape
    nu = control_ref.shape[2]
    both = trajs * width
    start = jnp.where(upper(step), got_ref[:1], init_ref[:1])
    for t in range(count):
        w = rows_times(start, map_ref[t], trajs) + offset_ref[t, :1]
        for j in range(trajs):
            state_ref[t : t + 1, j] = w[j : j + 1, j * width : (j + 1) * width]
            control_ref[t : t + 1, j] = w[j : j + 1, both + j * nu : both + (j + 1) * nu]
    sums = (own_ref[1:2] + got_ref[1:2]) / knots
    lane = lax.broadcasted_iota(jnp.int32, sums.shape, 1) // nu % trajs
    for j in range(trajs):
        decrease_ref[:, j : j + 1] = jnp.sum(jnp.where(lane == j, sums, 0.0), axis=1, keepdims=True)


def call(body, outs, *args, **named):
    return pl.pallas_call(
        body,
        out_shape=[
            jax.ShapeDtypeStruct(shape, F32) if isinstance(shape, tuple) else shape for shape in outs
        ],
        compiler_params=pltpu.CompilerParams(vmem_limit_bytes=32 * 1024 * 1024),
        **named,
    )(*args)


def halves(*shape):
    return jax.ShapeDtypeStruct(shape, jnp.bfloat16)


def without(body, at):
    @functools.wraps(body)
    def inner(*refs, **named):
        return body(*refs[:at], None, *refs[at:], **named)

    return inner


def unread(wanted, *values):
    return values if wanted else ()


def shards(dyn_a, dyn_b, gains, defects, state_grad, control_grad, cost_factor, control_factor, init_state):
    count, trajs, width, nu = dyn_b.shape
    devices = lax.axis_size("tm")
    knots = count * devices
    both, size = trajs * width, width + TAIL
    sizes = dict(trajs=trajs, width=width)
    steps = [1 << i for i in range(devices.bit_length() - 1)]

    def exchange(value, step, turn=1):
        apart = step ^ turn if step > 1 else step
        return lax.ppermute(value, "tm", [(i, i ^ apart) for i in range(devices)])

    stack = trajs * nu
    groups, up16 = count * stack // LANES, lambda n: -(-n // 16) * 16
    bt = jnp.swapaxes(dyn_b, 2, 3)
    inputs = (dyn_a, bt, gains, defects, state_grad, control_grad, cost_factor, control_factor)
    total, own, term, at, btp = call(
        functools.partial(block_kernel, knots),
        [(width + size, both), (count, 2, size, both), (size, both), (count, width, both), (count, nu, both)],
        *[pltpu.with_memory_space_constraint(x, pltpu.HBM) for x in inputs],
        in_specs=[pl.BlockSpec(memory_space=pltpu.HBM)] * len(inputs),
        scratch_shapes=[pltpu.VMEM(x.shape, F32) for x in inputs] + [pltpu.SemaphoreType.DMA((len(inputs),))],
    )
    suffix, = call(functools.partial(suffix_kernel, **sizes), [(count - 1, 2, size, both)], own)
    turned = (count, 2 * LANES, 2 * both)
    left, hess, cross, gain, bd, ad, run_r, control, init = call(
        functools.partial(prepare_kernel, knots),
        [halves(count, up16(nu + TAIL + width), 2 * both), halves(*turned), halves(*turned),
         halves(groups, *turned[1:]), (count, stack, both), (count, size, both), (nu, LANES), (stack, count),
         (TAIL, both)],
        at, btp, defects, control_grad, control_factor, init_state,
    )
    got = exchange(total, steps[0])
    total, after = call(
        functools.partial(without(value_step_kernel, 3), steps[0], **sizes),
        [(width + size, both), (2, size, both)], total, got
    )
    for i, step in enumerate(steps[1:-2]):
        got = exchange(total, step)
        total, after = call(
            functools.partial(value_step_kernel, step, **sizes), [(width + size, both), (2, size, both)],
            total, got, after, *unread(i == 0, init),
        )
    got = exchange(total, steps[-2], turn=0)
    value, = call(
        functools.partial(value_last_kernel, steps[-2], **sizes), [(size, both)], total, got, term, suffix
    )
    reach = call(
        functools.partial(reach_kernel, steps[-2], **sizes),
        [halves(count, up16(nu + TAIL), 2 * both), halves(*turned), halves(*turned), (count, stack, both),
         (groups, nu, LANES), (count, stack, LANES)],
        suffix, got, after, left, hess, cross, bd, run_r, control,
    )
    value = exchange(value, steps[-1])
    total, own, half, q = call(
        functools.partial(solve_kernel, steps[-1]),
        [(size, both), (count, size, both), (groups, size, LANES), (groups, nu, LANES)],
        term, value, *reach, gain, ad,
    )
    wide = both + -(-stack // LANES) * LANES
    new_gains, feedforward, maps = call(
        functools.partial(expand_kernel, **sizes),
        [(count, trajs, nu, width), (count, trajs, nu), (count, size, wide)], own, half, q,
    )
    seen = []
    for step in steps[:-2]:
        body = state_step_kernel if seen else without(state_step_kernel, 3)
        got = exchange(total, step)
        total, after = call(
            functools.partial(body, step, **sizes), [(size, both), (size, both)], total, got, *seen
        )
        seen = [after]
    got = exchange(total, steps[-2])
    sent, = call(
        functools.partial(state_last_kernel, steps[-2], **sizes), [(TAIL, both)], total, got, init, maps
    )
    maps, offsets = call(
        functools.partial(reach_state_kernel, steps[-2], **sizes, nu=nu),
        [halves(count, width, 2 * wide), (count, TAIL, wide)], maps, got, *seen,
    )
    got = exchange(sent, steps[-1])
    states, controls, decrease = call(
        functools.partial(rollout_kernel, knots, steps[-1]),
        [(count, trajs, width), (count, trajs, nu), (1, trajs)],
        sent, got, init, maps, offsets,
    )
    return new_gains, feedforward, states, controls, decrease.reshape(trajs)


def solution(mesh):
    in_specs = (
        P("tm", "grp", None, None),
        P("tm", "grp", None, None),
        P("tm", "grp", None, None),
        P("tm", "grp", None),
        P("tm", "grp", None),
        P("tm", "grp", None),
        P(),
        P(),
        P("grp", None),
    )
    out_specs = (
        P("tm", "grp", None, None),
        P("tm", "grp", None),
        P("tm", "grp", None),
        P("tm", "grp", None),
        P("grp"),
    )
    return jax.shard_map(shards, mesh=mesh, in_specs=in_specs, out_specs=out_specs, check_vma=False)
```

```python
import functools
import math

import jax
import jax.numpy as jnp
from jax import lax
from jax.experimental import pallas as pl
from jax.experimental.pallas import tpu as pltpu
from jax.sharding import PartitionSpec as P

F32 = jnp.float32
LANES = 128
TAIL = 8


def lane_block(shape, size):
    return lax.broadcasted_iota(jnp.int32, shape, 1) // size


def spread(pair, trajs):
    block = lane_block(pair.shape, pair.shape[1] // trajs)
    return jnp.concatenate([jnp.where(block == j, pair, 0.0) for j in range(trajs)], axis=0)


def split(x):
    high = x.astype(jnp.bfloat16)
    low = (x - high.astype(F32)).astype(jnp.bfloat16)
    return high, low


def left_of(x):
    return jnp.concatenate(split(x), axis=1)


def right_of(x, flip=False):
    depth, wide = (1, 0) if flip else (0, 1)
    both = jnp.concatenate(split(x), axis=wide)
    return jnp.concatenate([both, both], axis=depth)


def product_of(left, right, flip=False):
    dims = (((1,), (1 if flip else 0,)), ((), ()))
    w = lax.dot_general(left, right, dims, preferred_element_type=F32)
    full = w.shape[1] // 2
    return w[:, :full] + w[:, full:]


def prod(left, right, flip=False):
    wide = 0 if flip else 1
    columns = right.shape[wide]
    if columns % LANES:
        shape = list(right.shape)
        shape[wide] = -columns % LANES
        right = jnp.concatenate([right, jnp.zeros(shape, F32)], axis=wide)
    if left.shape[1] % LANES:
        rows, full = left.shape[0], right.shape[wide]
        dims = (((1,), (1 if flip else 0,)), ((), ()))
        w = lax.dot_general(
            jnp.concatenate(split(left), axis=0), jnp.concatenate(split(right), axis=wide), dims,
            preferred_element_type=F32,
        )
        w = w[:rows] + w[rows:]
        w = w[:, :full] + w[:, full:]
    else:
        w = product_of(left_of(left), right_of(right, flip), flip)
    return w[:, :columns]


def tail_of(row):
    shape = (TAIL, row.shape[1])
    return jnp.where(lax.broadcasted_iota(jnp.int32, shape, 0) == 0, jnp.broadcast_to(row, shape), 0.0)


def alone(tail):
    return jnp.where(lax.broadcasted_iota(jnp.int32, tail.shape, 0) == 0, tail, 0.0)


def with_second(tail, row):
    return jnp.where(lax.broadcasted_iota(jnp.int32, tail.shape, 0) == 1, jnp.broadcast_to(row, tail.shape), tail)


def one_piece(x, y, width):
    return jnp.concatenate([x[:width], y[:width], with_second(x[width:], y[width : width + 1])], axis=0)


def two_pieces(sent, width):
    tail = sent[2 * width :]
    return join(sent[:width], alone(tail)), join(sent[width : 2 * width], tail_of(tail[1:2]))


def join(matrix, tail):
    return jnp.concatenate([matrix, tail], axis=0)


def apply_values(maps, later, trajs, width):
    ws = [prod(late, spread(x[:width], trajs), flip=True) for (x, _), late in zip(maps, later)]
    zs = [prod(x, spread(w[:width], trajs)) + y for (x, y), w in zip(maps, ws)]
    return [join(z[:width], z[width:] + w[width:]) for z, w in zip(zs, ws)]


def compose_states(pairs, trajs, width):
    zs = [prod(first, spread(second[:width], trajs)) for first, second in pairs]
    return [join(z[:width], z[width:] + second[width:]) for z, (_, second) in zip(zs, pairs)]


def compose_values(pairs, trajs, width):
    ws = [prod(second[1], spread(first[0][:width], trajs), flip=True) for first, second in pairs]
    xs = compose_states([(first[0], second[0]) for first, second in pairs], trajs, width)
    zs = [prod(first[0], spread(w[:width], trajs)) + first[1] for (first, _), w in zip(pairs, ws)]
    return [(x, join(z[:width], z[width:] + w[width:])) for x, z, w in zip(xs, zs, ws)]


def fold(items, joined):
    while len(items) > 1:
        rest = items[len(items) // 2 * 2 :]
        items = joined([(items[i], items[i + 1]) for i in range(0, len(items) - 1, 2)]) + rest
    return items[0]


def prefixes(items, joined):
    items, step = list(items), 1
    while step < len(items):
        late = [i for i in range(len(items)) if i // step % 2]
        for i, joint in zip(late, joined([(items[i // step * step - 1], items[i]) for i in late])):
            items[i] = joint
        step *= 2
    return items


def identity_pair(width, trajs):
    rows = lax.broadcasted_iota(jnp.int32, (width, width * trajs), 0)
    lanes = lax.broadcasted_iota(jnp.int32, (width, width * trajs), 1)
    return jnp.where(rows == lanes % width, 1.0, 0.0)


def side_by_side(rows, trajs):
    return jnp.concatenate([rows[:, j] for j in range(trajs)], axis=1)


def term_of(cost_factor, trajs):
    width = cost_factor.shape[0]
    return prod(cost_factor, jnp.concatenate([cost_factor] * trajs, axis=0), flip=True) + identity_pair(width, trajs)


def paired(parts):
    return jnp.concatenate([parts[j] for j in range(parts.shape[0])], axis=1)


def block_kernel(knots, *refs):
    sources, (total_ref, own_ref, term_ref, at_ref, btp_ref), held, sems = refs[:8], refs[8:13], refs[13:21], refs[21]
    copies = [pltpu.make_async_copy(a, b, sems.at[i]) for i, (a, b) in enumerate(zip(sources, held))]
    order = (7, 2, 1, 6, 3, 4, 5, 0)
    for i in order:
        copies[i].start()
    a_ref, bt_ref, g_ref, d_ref, sg_ref, cg_ref, cf_ref, rf_ref = held
    count, trajs, nu, width = bt_ref.shape
    both = trajs * width
    scale = 1.0 / math.sqrt(knots)
    rows = lax.broadcasted_iota(jnp.int32, (nu, nu), 0)
    lanes = lax.broadcasted_iota(jnp.int32, (nu, nu), 1)
    for c in copies:
        c.wait()
    root = jnp.concatenate([jnp.where(rows == lanes, 1.0, 0.0), rf_ref[...]], axis=1)
    root = spread(jnp.concatenate([root] * trajs, axis=1), trajs)
    pushed = []
    for t in range(count):
        gt = g_ref[t].reshape(trajs * nu, width).T
        btp = paired(bt_ref[t])
        btp_ref[t] = btp
        pushed.append(prod(gt, jnp.concatenate([spread(btp, trajs), root], axis=1)))
    term = term_of(cf_ref[...], trajs)
    run_q = term / knots
    term_ref[...] = join(term, jnp.zeros((TAIL, both), F32))
    drift = side_by_side(d_ref[...], trajs) * scale
    grad = side_by_side(sg_ref[...], trajs) * scale
    cg = cg_ref[...]
    nothing = jnp.zeros((count, nu), F32)
    control = jnp.concatenate([piece for j in range(trajs) for piece in (cg[:, j], nothing)], axis=1)
    zs = [w[:, both:] for w in pushed]
    ys = [prod(join(z, tail_of(control[t : t + 1])), spread(z, trajs), flip=True) for t, z in enumerate(zs)]
    ys = [y + join(run_q, tail_of(grad[t : t + 1])) for t, y in enumerate(ys)]
    maps = []
    for t, (w, y) in enumerate(zip(pushed, ys)):
        at = a_ref[t].reshape(both, width).T
        at_ref[t] = at
        x = join(at + w[:, :both], tail_of(drift[t : t + 1]))
        own_ref[t, 0] = x
        own_ref[t, 1] = y
        maps.append((x, y))
    befores = prefixes([x for x, _ in maps], lambda pairs: compose_states(pairs, trajs, width))
    nothing = jnp.zeros_like(maps[0][1])
    parts = apply_values([(x, nothing) for x in befores[:-1]], [y for _, y in maps[1:]], trajs, width)
    total_ref[...] = one_piece(befores[-1], functools.reduce(jnp.add, parts, maps[0][1]), width)


def suffix_kernel(own_ref, *refs, trajs, width):
    out_ref, count = refs[-1], own_ref.shape[0]
    maps = [(own_ref[t, 0], own_ref[t, 1]) for t in reversed(range(1, count))]
    done = prefixes(maps, lambda pairs: compose_values([(b, a) for a, b in pairs], trajs, width))
    for i, (x, y) in enumerate(done):
        out_ref[count - 2 - i, 0] = x
        out_ref[count - 2 - i, 1] = y


def prepare_kernel(
    knots, at_ref, btp_ref, d_ref, cg_ref, rf_ref, x_ref,
    left_ref, hess_ref, cross_ref, gain_ref, bd_ref, ad_ref, run_r_ref, control_ref, init_ref,
):
    count, nu, both = btp_ref.shape
    trajs, width = x_ref.shape
    stack = trajs * nu
    group = LANES // stack
    init_ref[...] = tail_of(jnp.concatenate([x_ref[j : j + 1] for j in range(trajs)], axis=1))
    drift = side_by_side(d_ref[...], trajs) * (1.0 / math.sqrt(knots))
    control_ref[...] = side_by_side(cg_ref[...], trajs).T
    rf = rf_ref[...]
    rows = lax.broadcasted_iota(jnp.int32, (nu, nu), 0)
    lanes = lax.broadcasted_iota(jnp.int32, (nu, nu), 1)
    run_r = prod(rf, rf, flip=True) + jnp.where(rows == lanes, 1.0, 0.0)
    run_r_ref[...] = jnp.concatenate([run_r] * (LANES // nu), axis=1)
    spare = jnp.zeros((left_ref.shape[1] - nu - TAIL - width, both), F32)
    bds = []
    for t in range(count):
        at, btp = at_ref[t], btp_ref[t]
        bd = spread(btp, trajs)
        bds.append(bd)
        tail = tail_of(drift[t : t + 1])
        left_ref[t] = left_of(jnp.concatenate([btp, tail, at, spare], axis=0))
        hess_ref[t] = placed(bd, t % group, group)
        cross_ref[t] = right_of(over(at), flip=True)
        bd_ref[t] = bd
        ad_ref[t] = join(at, tail)
        if len(bds) == group:
            gain_ref[t // group] = right_of(jnp.concatenate(bds, axis=0))
            bds = []


def placed(bd, at, group):
    return right_of(jnp.concatenate([bd if i == at else jnp.zeros_like(bd) for i in range(group)], axis=0), flip=True)


def over(matrix):
    return jnp.concatenate([matrix, jnp.zeros((-matrix.shape[0] % LANES, matrix.shape[1]), F32)], axis=0)


def reach_kernel(
    step, suffix_ref, got_ref, seen_ref, left_ref, hess_ref, cross_ref, bd_ref, run_r_ref, control_ref,
    value_out, hess_out, cross_out, bd_out, hess_base, cross_base, *, trajs, width,
):
    count, nu = left_ref.shape[0], run_r_ref.shape[0]
    group = count // hess_base.shape[0]
    seen, got = (seen_ref[0], seen_ref[1]), two_pieces(got_ref[...], width)
    after, = compose_values([(seen, got)], trajs, width)
    seen = tuple(jnp.where(upper(step), a, b) for a, b in zip(seen, after))
    maps = compose_values([((suffix_ref[t, 0], suffix_ref[t, 1]), seen) for t in range(count - 1)], trajs, width)
    maps.append(seen)
    both = trajs * width
    rows = value_out.shape[1]
    firsts = [product_of(left_ref[t], right_of(spread(x[:width], trajs))) for t, (x, _) in enumerate(maps)]
    us = [product_of(left_ref[t, :rows], right_of(spread(y[:width], trajs))) for t, (_, y) in enumerate(maps)]
    hesses = [product_of(left_of(u[:nu]), hess_ref[t], flip=True) for t, u in enumerate(us)]
    crosses = [product_of(left_of(spread(u[:nu], trajs)), cross_ref[t], flip=True) for t, u in enumerate(us)]
    lin_lane = lax.broadcasted_iota(jnp.int32, crosses[0].shape, 1) == width
    spare = jnp.zeros((rows - nu - TAIL, both), F32)
    for t, (w, (x, y)) in enumerate(zip(firsts, maps)):
        bd = spread(w[:nu], trajs)
        value_out[t] = left_of(jnp.concatenate([w[:nu], w[nu : nu + TAIL] + x[width:], spare], axis=0))
        hess_out[t] = placed(bd, t % group, group)
        cross_out[t] = right_of(over(w[nu + TAIL : nu + TAIL + width]), flip=True)
        bd_out[t] = bd
        vector = us[t][nu : nu + 1] + y[width : width + 1]
        lin = jnp.sum(bd_ref[t] * vector, axis=1, keepdims=True) + control_ref[:, t : t + 1]
        cross_base[t] = jnp.where(lin_lane, lin, crosses[t])
    for g in range(count // group):
        hess_base[g] = functools.reduce(jnp.add, hesses[g * group : (g + 1) * group], run_r_ref[...])


def upper(step):
    return lax.rem(lax.axis_index("tm") // step, 2) == 1


def value_step_kernel(step, own_ref, got_ref, seen_ref, *refs, trajs, width):
    total_ref, next_ref = refs[-2:]
    up = upper(step)
    own, got = own_ref[...], got_ref[...]
    first, second = two_pieces(jnp.where(up, got, own), width), two_pieces(jnp.where(up, own, got), width)
    got = two_pieces(got, width)
    if seen_ref is None:
        seen = (join(identity_pair(width, trajs), jnp.zeros((TAIL, trajs * width), F32)), jnp.zeros_like(got[1]))
        (x, y), = compose_values([(first, second)], trajs, width)
        after = got
    else:
        seen = (seen_ref[0], seen_ref[1])
        (x, y), after = compose_values([(first, second), (seen, got)], trajs, width)
    total_ref[...] = one_piece(x, y, width)
    next_ref[0] = jnp.where(up, seen[0], after[0])
    next_ref[1] = jnp.where(up, seen[1], after[1])


def value_last_kernel(step, own_ref, got_ref, term_ref, *refs, trajs, width):
    up = upper(step)
    own, got = own_ref[...], got_ref[...]
    first, second = two_pieces(jnp.where(up, got, own), width), two_pieces(jnp.where(up, own, got), width)
    total, = compose_values([(first, second)], trajs, width)
    refs[-1][...], = apply_values([total], [term_ref[...]], trajs, width)


def factors(packs, size):
    block, step = 8, 4
    rows = lax.broadcasted_iota(jnp.int32, (block, LANES), 0)
    lanes = lax.broadcasted_iota(jnp.int32, (block, LANES), 1)
    inner = lanes % size
    first = lanes - inner
    packs = [[pack[i : i + block] for i in range(0, size, block)] for pack in packs]
    ws = [[jnp.zeros((block, LANES), F32) for _ in pack] for pack in packs]
    qs = [list(w) for w in ws]
    for k in range(0, size, step):
        at, r = k // block, k % block
        inside = (inner >= k) & (inner < k + step)
        known = inner[:1] < k + step
        for number, pack in enumerate(packs):
            columns = {
                i: [jnp.take_along_axis(pack[i], first + (k + j), axis=1) for j in range(step)]
                for i in range(at, len(pack))
            }
            p = [[columns[at][j][r + i : r + i + 1] for j in range(step)] for i in range(step)]
            z = [
                jnp.where(inside[:1], jnp.where(inner[:1] == k + i, 1.0, 0.0), pack[at][r + i : r + i + 1])
                for i in range(step)
            ]
            for i in range(step):
                ws[number][at] = jnp.where(rows == r + i, jnp.where(known, z[i], 0.0), ws[number][at])
            inverse = []
            for i in range(step):
                inverse.append(1.0 / p[i][i])
                for j in range(i + 1, step):
                    ratio = p[j][i] * inverse[i]
                    for c in range(i + 1, step):
                        p[j][c] = p[j][c] - ratio * p[i][c]
                    z[j] = z[j] - ratio * z[i]
            q = [None] * step
            for i in reversed(range(step)):
                v = z[i]
                for j in range(i + 1, step):
                    v = v - p[i][j] * q[j]
                q[i] = v * inverse[i]
            for i in range(step):
                qs[number][at] = jnp.where(rows == r + i, jnp.where(known, q[i], 0.0), qs[number][at])
            for i in range(at if r + step < block else at + 1, len(pack)):
                y = jnp.where(inside, 0.0, pack[i])
                for j in range(step):
                    y = y - columns[i][j] * q[j]
                pack[i] = y
    return [(jnp.concatenate(w, axis=0), jnp.concatenate(q, axis=0)) for w, q in zip(ws, qs)]


def solve_kernel(
    step, term_ref, end_ref, value_ref, hess_ref, cross_ref, bd_ref, hess_base, cross_base, gain_ref, ad_ref,
    total_ref, own_ref, half_ref, q_ref,
):
    count, stack, both = bd_ref.shape
    size = ad_ref.shape[1]
    groups, nu, _ = hess_base.shape
    width = size - TAIL
    trajs, group = both // width, count // groups
    rows = value_ref.shape[1]
    lin_lane = lax.broadcasted_iota(jnp.int32, (stack, LANES), 1) == width

    end = jnp.where(upper(step), term_ref[...], end_ref[...])
    w = product_of(value_ref[...].reshape(count * rows, 2 * both), right_of(spread(end[:width], trajs)))
    us = [w[t * rows : t * rows + nu] for t in range(count)]
    hesses = [product_of(left_of(u), hess_ref[t], flip=True) for t, u in enumerate(us)]
    hesses = [functools.reduce(jnp.add, hesses[g * group : (g + 1) * group], hess_base[g]) for g in range(groups)]
    pairs = factors(hesses, nu)
    crosses = [product_of(left_of(spread(u, trajs)), cross_ref[t], flip=True) for t, u in enumerate(us)]
    systems = []
    for t, cross in enumerate(crosses):
        vector = w[t * rows + nu : t * rows + nu + 1] + end[width : width + 1]
        lin = jnp.sum(bd_ref[t] * vector, axis=1, keepdims=True)
        systems.append(jnp.where(lin_lane, lin, cross) + cross_base[t])

    flats = [jnp.concatenate(systems[t : t + group], axis=0).T[:size] for t in range(0, count, group)]
    lefts = [left_of(flat) for flat in flats]
    lanes = lax.broadcasted_iota(jnp.int32, (1, LANES), 1)
    spreads = [(spread(w, LANES // nu), spread(q, LANES // nu)) for w, q in pairs]
    halves = [product_of(left, right_of(w, flip=True), flip=True) for left, (w, _) in zip(lefts, spreads)]
    pushes = [product_of(left_of(q), gain_ref[g]) for g, (_, q) in enumerate(spreads)]
    maps = []
    for g, half in enumerate(halves):
        left = left_of(half)
        for i in range(group):
            mine = pushes[g][i * stack : (i + 1) * stack]
            pieces = [mine if k == i else jnp.zeros_like(mine) for k in range(group)]
            maps.append(ad_ref[g * group + i] - product_of(left, right_of(jnp.concatenate(pieces, axis=0))))
    decrease = jnp.zeros((1, LANES), F32)
    for g, (half, flat) in enumerate(zip(halves, flats)):
        half_ref[g] = half
        q_ref[g] = pairs[g][1]
        feed = -prod(half[width:], spreads[g][1])[:1]
        feed_columns = jnp.broadcast_to(feed, (TAIL, LANES)).T
        weights = jnp.zeros((nu, LANES), F32)
        for at in range(LANES // nu):
            column = feed_columns[at * nu : (at + 1) * nu, :1]
            weights = jnp.where((lanes >= at * nu) & (lanes < (at + 1) * nu), column, weights)
        pushed = jnp.sum(weights * hesses[g], axis=0, keepdims=True)
        decrease = decrease + feed * flat[width : width + 1] + 0.5 * (feed * pushed)
    total = fold(maps, lambda pairs: compose_states(pairs, trajs, width))
    total_ref[...] = join(total[:width], with_second(total[width:], decrease))
    for t, m in enumerate(maps):
        own_ref[t] = m


def expand_kernel(
    own_ref, half_ref, q_ref, gain_ref, feed_ref, map_ref, *, trajs, width
):
    count, size, both = own_ref.shape
    groups, nu, _ = q_ref.shape
    group, stack = count // groups, trajs * nu
    gains = []
    kts = [-prod(half_ref[g], spread(q_ref[g], LANES // nu)) for g in range(groups)]
    for g, kt in enumerate(kts):
        spare = jnp.zeros((LANES - size, LANES), F32)
        natural = join(kt, spare).T
        for i in range(group):
            t = g * group + i
            gain_ref[t] = natural[i * stack : (i + 1) * stack, :width].reshape(trajs, nu, width)
            for j in range(trajs):
                at = i * stack + j * nu
                feed_ref[t : t + 1, j] = kt[width : width + 1, at : at + nu]
            gains.append(kt[:, i * stack : (i + 1) * stack])
    maps = [own_ref[t] for t in range(count - 1)]
    done = prefixes(maps, lambda pairs: compose_states(pairs, trajs, width))
    start = join(identity_pair(width, trajs), jnp.zeros((TAIL, both), F32))
    controls = [prod(m, spread(kt[:width], trajs)) for m, kt in zip(done, gains[1:])]
    controls = [join(u[:width], u[width:] + kt[width:]) for u, kt in zip(controls, gains[1:])]
    for t, (m, control) in enumerate(zip([start] + done, gains[:1] + controls)):
        map_ref[t] = jnp.concatenate([m, control, jnp.zeros((size, -stack % LANES), F32)], axis=1)


def reach_state_kernel(step, map_ref, got_ref, seen_ref, out_ref, offset_ref, *, trajs, width, nu):
    seen = seen_ref[...]
    got = join(got_ref[:width], alone(got_ref[width:]))
    after, = compose_states([(got, seen)], trajs, width)
    seen = jnp.where(upper(step), after, seen)
    rows = jnp.concatenate([seen[:, j * width : (j + 1) * width] for j in range(trajs)], axis=0)
    size, both = seen.shape
    tails = map_ref[:, width:]
    products = [prod(rows, map_ref[t, :width]) for t in range(map_ref.shape[0])]
    for t, w in enumerate(products):
        lane = lax.broadcasted_iota(jnp.int32, (size, w.shape[1]), 1)
        owner = jnp.where(lane < both, lane // width, (lane - both) // nu)
        full = w[:size]
        for j in range(1, trajs):
            full = jnp.where(owner >= j, w[j * size : (j + 1) * size], full)
        out_ref[t] = jnp.concatenate(split(full[:width]), axis=1)
        offset_ref[t] = full[width:] + tails[t]


def state_pair(step, own_ref, got_ref, width):
    up, own, got = upper(step), own_ref[...], got_ref[...]
    ride = own[width + 1 : width + 2] + got[width + 1 : width + 2]
    own, got = join(own[:width], alone(own[width:])), join(got[:width], alone(got[width:]))
    return (jnp.where(up, got, own), jnp.where(up, own, got)), got, ride


def state_step_kernel(step, own_ref, got_ref, seen_ref, total_ref, next_ref, *, trajs, width):
    pair, got, ride = state_pair(step, own_ref, got_ref, width)
    if seen_ref is None:
        seen = join(identity_pair(width, trajs), jnp.zeros((TAIL, trajs * width), F32))
        total, = compose_states([pair], trajs, width)
        after = got
    else:
        seen = seen_ref[...]
        total, after = compose_states([pair, (got, seen)], trajs, width)
    total_ref[...] = join(total[:width], with_second(total[width:], ride))
    next_ref[...] = jnp.where(upper(step), after, seen)


def state_last_kernel(step, own_ref, got_ref, init_ref, *refs, trajs, width):
    pair, _, ride = state_pair(step, own_ref, got_ref, width)
    total, = compose_states([pair], trajs, width)
    state = prod(init_ref[...], spread(total[:width], trajs)) + total[width:]
    refs[-1][...] = with_second(state, ride)


def rows_times(row, right, trajs):
    width = right.shape[0]
    rows = jnp.concatenate([row[:1, j * width : (j + 1) * width] for j in range(trajs)], axis=0)
    high = rows.astype(jnp.bfloat16).astype(F32)
    left = jnp.concatenate([high, rows - high], axis=0).astype(jnp.bfloat16)
    w = lax.dot_general(left, right, (((1,), (0,)), ((), ())), preferred_element_type=F32)
    w = w[:trajs] + w[trajs:]
    full = w.shape[1] // 2
    return w[:, :full] + w[:, full:]


def rollout_kernel(knots, step, own_ref, got_ref, init_ref, map_ref, offset_ref,
                   state_ref, control_ref, decrease_ref):
    count, trajs, width = state_ref.shape
    nu = control_ref.shape[2]
    both = trajs * width
    start = jnp.where(upper(step), got_ref[:1], init_ref[:1])
    for t in range(count):
        w = rows_times(start, map_ref[t], trajs) + offset_ref[t, :1]
        for j in range(trajs):
            state_ref[t : t + 1, j] = w[j : j + 1, j * width : (j + 1) * width]
            control_ref[t : t + 1, j] = w[j : j + 1, both + j * nu : both + (j + 1) * nu]
    sums = (own_ref[1:2] + got_ref[1:2]) / knots
    lane = lax.broadcasted_iota(jnp.int32, sums.shape, 1) // nu % trajs
    for j in range(trajs):
        decrease_ref[:, j : j + 1] = jnp.sum(jnp.where(lane == j, sums, 0.0), axis=1, keepdims=True)


def call(body, outs, *args, **named):
    return pl.pallas_call(
        body,
        out_shape=[
            jax.ShapeDtypeStruct(shape, F32) if isinstance(shape, tuple) else shape for shape in outs
        ],
        compiler_params=pltpu.CompilerParams(vmem_limit_bytes=32 * 1024 * 1024),
        **named,
    )(*args)


def halves(*shape):
    return jax.ShapeDtypeStruct(shape, jnp.bfloat16)


def without(body, at):
    @functools.wraps(body)
    def inner(*refs, **named):
        return body(*refs[:at], None, *refs[at:], **named)

    return inner


def unread(wanted, *values):
    return values if wanted else ()


def shards(dyn_a, dyn_b, gains, defects, state_grad, control_grad, cost_factor, control_factor, init_state):
    count, trajs, width, nu = dyn_b.shape
    devices = lax.axis_size("tm")
    knots = count * devices
    both, size = trajs * width, width + TAIL
    sizes = dict(trajs=trajs, width=width)
    steps = [1 << i for i in range(devices.bit_length() - 1)]

    def exchange(value, step, turn=1):
        apart = step ^ turn if step > 1 else step
        return lax.ppermute(value, "tm", [(i, i ^ apart) for i in range(devices)])

    stack = trajs * nu
    groups, up16 = count * stack // LANES, lambda n: -(-n // 16) * 16
    bt = jnp.swapaxes(dyn_b, 2, 3)
    inputs = (dyn_a, bt, gains, defects, state_grad, control_grad, cost_factor, control_factor)
    total, own, term, at, btp = call(
        functools.partial(block_kernel, knots),
        [(width + size, both), (count, 2, size, both), (size, both), (count, width, both), (count, nu, both)],
        *[pltpu.with_memory_space_constraint(x, pltpu.HBM) for x in inputs],
        in_specs=[pl.BlockSpec(memory_space=pltpu.HBM)] * len(inputs),
        scratch_shapes=[pltpu.VMEM(x.shape, F32) for x in inputs] + [pltpu.SemaphoreType.DMA((len(inputs),))],
    )
    suffix, = call(functools.partial(suffix_kernel, **sizes), [(count - 1, 2, size, both)], own)
    turned = (count, 2 * LANES, 2 * both)
    left, hess, cross, gain, bd, ad, run_r, control, init = call(
        functools.partial(prepare_kernel, knots),
        [halves(count, up16(nu + TAIL + width), 2 * both), halves(*turned), halves(*turned),
         halves(groups, *turned[1:]), (count, stack, both), (count, size, both), (nu, LANES), (stack, count),
         (TAIL, both)],
        at, btp, defects, control_grad, control_factor, init_state,
    )
    got = exchange(total, steps[0])
    total, after = call(
        functools.partial(without(value_step_kernel, 3), steps[0], **sizes),
        [(width + size, both), (2, size, both)], total, got
    )
    for i, step in enumerate(steps[1:-2]):
        got = exchange(total, step)
        total, after = call(
            functools.partial(value_step_kernel, step, **sizes), [(width + size, both), (2, size, both)],
            total, got, after, *unread(i == 0, init),
        )
    got = exchange(total, steps[-2], turn=0)
    value, = call(
        functools.partial(value_last_kernel, steps[-2], **sizes), [(size, both)], total, got, term, suffix
    )
    reach = call(
        functools.partial(reach_kernel, steps[-2], **sizes),
        [halves(count, up16(nu + TAIL), 2 * both), halves(*turned), halves(*turned), (count, stack, both),
         (groups, nu, LANES), (count, stack, LANES)],
        suffix, got, after, left, hess, cross, bd, run_r, control,
    )
    value = exchange(value, steps[-1])
    total, own, half, q = call(
        functools.partial(solve_kernel, steps[-1]),
        [(size, both), (count, size, both), (groups, size, LANES), (groups, nu, LANES)],
        term, value, *reach, gain, ad,
    )
    wide = both + -(-stack // LANES) * LANES
    new_gains, feedforward, maps = call(
        functools.partial(expand_kernel, **sizes),
        [(count, trajs, nu, width), (count, trajs, nu), (count, size, wide)], own, half, q,
    )
    seen = []
    for step in steps[:-2]:
        body = state_step_kernel if seen else without(state_step_kernel, 3)
        got = exchange(total, step)
        total, after = call(
            functools.partial(body, step, **sizes), [(size, both), (size, both)], total, got, *seen
        )
        seen = [after]
    got = exchange(total, steps[-2])
    sent, = call(
        functools.partial(state_last_kernel, steps[-2], **sizes), [(TAIL, both)], total, got, init, maps
    )
    maps, offsets = call(
        functools.partial(reach_state_kernel, steps[-2], **sizes, nu=nu),
        [halves(count, width, 2 * wide), (count, TAIL, wide)], maps, got, *seen,
    )
    got = exchange(sent, steps[-1])
    states, controls, decrease = call(
        functools.partial(rollout_kernel, knots, steps[-1]),
        [(count, trajs, width), (count, trajs, nu), (1, trajs)],
        sent, got, init, maps, offsets,
    )
    return new_gains, feedforward, states, controls, decrease.reshape(trajs)


def solution(mesh):
    in_specs = (
        P("tm", "grp", None, None),
        P("tm", "grp", None, None),
        P("tm", "grp", None, None),
        P("tm", "grp", None),
        P("tm", "grp", None),
        P("tm", "grp", None),
        P(),
        P(),
        P("grp", None),
    )
    out_specs = (
        P("tm", "grp", None, None),
        P("tm", "grp", None),
        P("tm", "grp", None),
        P("tm", "grp", None),
        P("grp"),
    )
    return jax.shard_map(shards, mesh=mesh, in_specs=in_specs, out_specs=out_specs, check_vma=False)
```
